256 devices in a mesh: dp: 32 (over z_hi, x, core), tensor: 8 (over y, z_lo).
Axes of the slice: x: 4, y: 4, z: 8 (z_hi: 4, z_lo: 2; z = z_hi * 2 + z_lo), core: 2. Of those that a mesh axis runs over, the one named last changes fastest.
Arguments:
- hidden_in: bfloat16 [16384, 4608], P('dp'), may hold values from -6 to 6
- kv_weight: bfloat16 [4608, 4096], P(None, 'tensor'), may hold values from -0.09375 to 0.09375
- kv_cotangent: bfloat16 [16384, 4096], P('dp', 'tensor'), may hold values from -6 to 6
- token_counts: int32 [32], P('dp'), may hold values from 256 to 512, as said below
- block_signs: int32 [4096], P('tensor'), may hold values from 0 to 1
- level_table: float32 [256], replicated, may hold values from 0.4 to 2.5
- level_index: int32 [32, 4608], P('tensor'), may hold values from 0 to 255
Outputs:
- input_grad: bfloat16 [16384, 4608], P('dp', 'tensor')
- kv_grad: bfloat16 [4608, 4096], P(None, 'tensor')
The draws below stay inside these ranges and needn't reach their ends.
Inputs may be any that keep to these rules, and one draw needn't show every extreme that they name: `token_counts`: slots of a replica at or beyond its count hold padding.
All inputs are finite; a program needn't handle non-finite values.
Results may differ from the reference program's by a relative error of at most 0.023.
Values may be sent and summed in bfloat16 or wider, within the bound.
A program may use at most 128 MiB of HBM per device.

```python
import math
import jax
import jax.numpy as jnp
from jax import lax

D = 4608
HEAD = 128
KVH_DEV = 2
LEVELS = 256
TOK_DEV = 512
KV_COLS = 4096
BLOCKS = 32
TOKENS = 16384
N_DP = 32
N_TENSOR = 8


def draw_token_counts(key, part):
    key = jax.random.fold_in(key, 11)
    counts = jax.random.randint(key, (N_DP,), TOK_DEV // 2, TOK_DEV + 1)
    chosen = jax.random.randint(jax.random.fold_in(key, 2), (), 0, N_DP)
    places = jnp.arange(N_DP, dtype=jnp.int32)
    counts = jnp.where(places == chosen, TOK_DEV, counts)
    counts = jnp.where(places == (chosen + 1) % N_DP, TOK_DEV // 2, counts)
    return counts.astype(jnp.int32)


def set_ends(drawn, own_key, least, high):
    longest = drawn.shape.index(max(drawn.shape))
    spots = []
    for shift in (0, 1):
        where = [jax.random.randint(jax.random.fold_in(own_key, axis), (), 0, length) for axis, length in enumerate(drawn.shape)]
        where[longest] = (where[longest] + shift) % drawn.shape[longest]
        spots.append(tuple(where))
    return drawn.at[spots[0]].set(least).at[spots[1]].set(high)


def block_scale(stream_key, shape, split, low, high):
    def one(position, parts):
        heights = jax.random.uniform(jax.random.fold_in(jax.random.fold_in(stream_key, 6), position), (parts,), jnp.float32, low / len(split), high / len(split))
        return jnp.repeat(jnp.exp(heights), shape[position] // parts).reshape((-1,) + (1,) * (len(shape) - position - 1))

    gain = one(*split[0])
    for cut in split[1:]:
        gain = gain * one(*cut)
    return gain


def gaussian(key, dims, deviation, bound, pieces=(), kind=jnp.bfloat16):
    values = jax.random.normal(key, dims, jnp.float32) * deviation
    if len(pieces) > 0:
        values = block_scale(key, dims, pieces, -0.22, 0.18) * values
    return jnp.clip(values, min=-bound, max=bound).astype(kind)


def setup_inputs(seed: int = 0) -> dict:
    key_list = jax.random.split(jax.random.key(seed), 8)
    return {
        "hidden_in": gaussian(key_list[0], (TOKENS, D), 1.0, 6.0, ((0, 32),)),
        "kv_weight": gaussian(key_list[1], (D, KV_COLS), KV_COLS ** -0.5, 0.09375, ((1, 8),)),
        "kv_cotangent": gaussian(key_list[2], (TOKENS, KV_COLS), 1.0, 6.0, ((0, 32), (1, 8))),
        "token_counts": draw_token_counts(jax.random.fold_in(key_list[7], 71), 0),
        "block_signs": set_ends(jax.random.randint(key_list[4], (KV_COLS,), 0, 2), jax.random.fold_in(key_list[4], 1), 0, 1).astype(jnp.int32),
        "level_table": jnp.clip(jnp.exp(jax.random.uniform(key_list[5], (LEVELS,), jnp.float32, math.log(0.4), math.log(2.5))), 0.4, 2.5),
        "level_index": set_ends(jax.random.randint(key_list[6], (BLOCKS, D), 0, LEVELS), jax.random.fold_in(key_list[6], 1), 0, LEVELS - 1).astype(jnp.int32),
    }


def sylvester(order):
    indices = jnp.arange(order, dtype=jnp.int32)
    common = jnp.bitwise_and(indices[:, None], indices[None, :])
    parity = jnp.zeros((order, order), jnp.int32)
    for bit_index in range(order.bit_length() - 1):
        parity = parity + jnp.bitwise_and(jnp.right_shift(common, bit_index), 1)
    return jnp.where(parity % 2 == 0, 1.0, -1.0).astype(jnp.float32)

def rotate_blocks(values, hadamard):
    return jnp.einsum('rjk,kl->rjl', values, hadamard, precision=lax.Precision.HIGHEST) / math.sqrt(HEAD)

def reference(hidden_in, kv_weight, kv_cotangent, token_counts, block_signs, level_table, level_index):
    group_cols = 2 * KVH_DEV * HEAD
    all_cols = kv_weight.shape[1]
    block_count = all_cols // HEAD
    slot_index = jnp.arange(TOK_DEV, dtype=jnp.int32)
    valid_rows = (slot_index[None, :] < token_counts[:, None]).reshape(-1)
    masked = jnp.where(valid_rows[:, None], kv_cotangent, jnp.zeros_like(kv_cotangent))
    running = jnp.zeros((masked.shape[0], D), jnp.float32)
    for part_index in range(N_TENSOR):
        first_col = part_index * group_cols
        partial_term = jnp.dot(masked[:, first_col:first_col + group_cols], kv_weight[:, first_col:first_col + group_cols].T, preferred_element_type=jnp.float32)
        running = running + lax.optimization_barrier(partial_term.astype(jnp.bfloat16)).astype(jnp.float32)
    input_grad = running.astype(jnp.bfloat16)
    sign_values = (2 * block_signs - 1).astype(jnp.float32)
    hadamard = sylvester(HEAD)
    bounds = level_table[level_index].T

    def replica(summed, inputs):
        replica_rows, replica_cot = inputs
        gradient = jnp.dot(replica_rows.T, replica_cot, preferred_element_type=jnp.float32) / math.sqrt(TOK_DEV)
        rotated = rotate_blocks((gradient * sign_values).reshape(D, block_count, HEAD), hadamard)
        encoded = jnp.clip(rotated, -bounds[..., None], bounds[..., None]).astype(jnp.bfloat16)
        widened = lax.optimization_barrier(encoded).astype(jnp.float32)
        return (summed + widened.reshape(D, all_cols), None)
    summed, _ = lax.scan(replica, jnp.zeros((D, all_cols), jnp.float32), (hidden_in.reshape(N_DP, TOK_DEV, D), masked.reshape(N_DP, TOK_DEV, all_cols)))
    requant = (summed / math.sqrt(N_DP)).astype(jnp.bfloat16)
    widened = lax.optimization_barrier(requant).astype(jnp.float32)
    decoded = rotate_blocks(widened.reshape(D, block_count, HEAD), hadamard).reshape(D, all_cols) * sign_values
    return (input_grad, decoded.astype(jnp.bfloat16))
```

```python
import functools
import math

import jax
import jax.numpy as jnp
from jax import lax
from jax.experimental import pallas as pl
from jax.experimental.pallas import tpu as pltpu
from jax.sharding import PartitionSpec as P

MESH = pl.DeviceIdType.MESH
F32 = jnp.float32
BF16 = jnp.bfloat16
HEAD = 128
NX, NZ, NY = 4, 4, 4

KV_WAVES = (1, 2, 2, 2, 2)
Y_WAVES = (128, 128, 128, 128, 64)


def starts(sizes):
    out, at = [], 0
    for size in sizes:
        out.append(at)
        at += size
    return tuple(out)


KV_AT = starts(KV_WAVES)
Y_AT = starts(Y_WAVES)


def order():
    plan = []
    step = 4.6
    for w in range(len(KV_WAVES)):
        t = 0.0 if w == 0 else 2.0 + step * w
        for name, late in (
            ("encode", 0.0), ("pair", 3.0), ("x_mid", 6.5), ("x_end", 9.5), ("z_mid", 12.5), ("z_end", 15.5),
            ("z_pass", 18.5), ("x_own", 21.0), ("x_pass", 25.0), ("pair_last", 29.0),
        ):
            plan.append((t + late, name, w))
    step = 7.7
    for v in range(len(Y_WAVES)):
        t = 1.0 if v == 0 else 3.0 + step * v
        for name, late in (("partial", 0.0), ("y_mid", 5.0), ("y_end", 10.5), ("zl_end", 14.0)):
            plan.append((t + late, name, v))
    plan.sort()
    return [(name, w) for _, name, w in plan]


def rows_of(at, size):
    return pl.ds(pl.multiple_of(at, 16), size)


def add_rows(out, out_at, terms, size, block=32):
    block = min(block, size)

    def step(i, _):
        total = None
        for ref, at in terms:
            value = ref[rows_of(at + i * block, block), :].astype(F32)
            total = value if total is None else total + value
        out[rows_of(out_at + i * block, block), :] = total.astype(BF16)
        return 0

    lax.fori_loop(0, size // block, step, 0)


def kernel(
    count, hidden_hbm, weight_hbm, cot_hbm, signs_hbm, table_hbm, index_hbm,
    grad_out, input_out,
    hidden, weight, masked, signs, table, index, bt, enc, pair_in, summed,
    x_mid_in, x_in, x_sum, z_mid_in, z_in, part, y_mid_in, y_in, y_sum, zl_in,
    local_sem, send_sem, recv_sem,
):
    dp, tensor = lax.axis_index("dp"), lax.axis_index("tensor")
    zh, x, core = dp // 8, (dp // 2) % 4, dp % 2
    y, zl = tensor // 2, tensor % 2

    def dp_of(zh_, x_, core_):
        return ((zh_ % 4) * 4 + (x_ % 4)) * 2 + core_

    def at_dp(zh_, x_, core_):
        return (dp_of(zh_, x_, core_), tensor)

    peer = at_dp(zh, x, 1 - core)
    x_next, x_prev = at_dp(zh, x + 1, core), at_dp(zh, x + 3, core)
    z_next, z_prev = at_dp(zh + 1, x, core), at_dp(zh + 3, x, core)
    y_next, y_prev = (dp, ((y + 1) % 4) * 2 + zl), (dp, ((y + 3) % 4) * 2 + zl)
    zl_peer = (dp, y * 2 + 1 - zl)
    neighbours = (peer, x_next, x_prev, z_next, z_prev, y_next, y_prev, zl_peer)

    barrier = pltpu.get_barrier_semaphore()
    for device in neighbours:
        pl.semaphore_signal(barrier, inc=1, device_id=device, device_id_type=MESH)

    used = [0]
    local_used = [0]
    sent = []

    def load(src, dst):
        copy = pltpu.make_async_copy(src, dst, local_sem.at[local_used[0]])
        local_used[0] += 1
        copy.start()
        return copy

    def send(src, dst, device):
        copy = pltpu.make_async_remote_copy(
            src_ref=src, dst_ref=dst, send_sem=send_sem.at[used[0]], recv_sem=recv_sem.at[used[0]],
            device_id=device, device_id_type=MESH,
        )
        used[0] += 1
        copy.start()
        sent.append(copy)
        return copy

    cot_load = load(cot_hbm, masked)
    small_loads = [load(signs_hbm, signs), load(table_hbm, table), load(index_hbm, index)]
    hidden_loads, weight_loads = [], []

    def load_hidden(w):
        lanes = pl.ds(KV_AT[w] * 512, KV_WAVES[w] * 512)
        hidden_loads.append(load(hidden_hbm.at[:, lanes], hidden.at[:, lanes]))

    def load_weight(v):
        size = Y_WAVES[v]
        weight_loads.append([
            load(weight_hbm.at[pl.ds(t * 576 + Y_AT[v], size), :], weight.at[pl.ds(8 * Y_AT[v] + t * size, size), :])
            for t in range(8)
        ])

    for w in range(max(len(KV_WAVES), len(Y_WAVES))):
        if w < len(KV_WAVES):
            load_hidden(w)
        if w < len(Y_WAVES):
            load_weight(w)

    row_i = lax.broadcasted_iota(jnp.int32, (HEAD, HEAD), 0)
    col_i = lax.broadcasted_iota(jnp.int32, (HEAD, HEAD), 1)
    common = row_i & col_i
    common = common ^ (common >> 4)
    common = common ^ (common >> 2)
    common = common ^ (common >> 1)
    hadamard = (1 - 2 * (common & 1)).astype(F32)

    cot_load.wait()
    tokens = lax.broadcasted_iota(jnp.int32, (512, 512), 0)
    masked[...] = jnp.where(tokens < count[0], masked[...].astype(F32), 0.0).astype(BF16)
    for copy in small_loads:
        copy.wait()
    sign_row = (2 * signs[...] - 1).astype(F32)
    for j in range(4):
        lanes = pl.ds(j * HEAD, HEAD)
        turned = (hadamard * sign_row[:, j * HEAD:(j + 1) * HEAD]).astype(BF16)
        bt[lanes, :] = (
            lax.dot_general(turned, masked[:, lanes], (((1,), (1,)), ((), ())), preferred_element_type=F32)
            * (1.0 / 256.0)
        ).astype(BF16)

    waiting = {}

    def encode(w):
        hidden_loads[w].wait()

        def tile(i, _):
            at = pl.multiple_of((KV_AT[w] + i) * 512, 512)
            value = jnp.dot(bt[...], hidden[:, pl.ds(at, 512)], preferred_element_type=F32)
            low = jnp.broadcast_to(table[:, 0:128], (4, 128))
            high = jnp.broadcast_to(table[:, 128:256], (4, 128))
            bounds = []
            for k in range(4):
                ids = index[:, pl.ds(at + k * 128, 128)]
                first = jnp.take_along_axis(low, ids & 127, axis=1, mode="promise_in_bounds")
                second = jnp.take_along_axis(high, ids & 127, axis=1, mode="promise_in_bounds")
                bounds.append(jnp.where(ids >= 128, second, first))
            bound = jnp.concatenate(bounds, axis=1)
            for j in range(4):
                limit = bound[j:j + 1, :]
                clipped = jnp.clip(value[j * HEAD:(j + 1) * HEAD], -limit, limit).astype(BF16)
                enc[pl.ds(at, 512), pl.ds(j * HEAD, HEAD)] = clipped.T
            return 0

        lax.fori_loop(0, KV_WAVES[w], tile, 0)

    def own_rows(w, core_):
        g = KV_WAVES[w]
        return KV_AT[w] * 512 + core_ * 256 * g, 256 * g

    def pair_send(w):
        at, size = own_rows(w, 1 - core)
        waiting["pair", w] = send(
            enc.at[rows_of(at, size), :], pair_in.at[pl.ds(KV_AT[w] * 256, size), :], peer
        )

    class Axis:
        def __init__(self, name, place, following, previous, source, mid_in, into, half, by_lanes):
            self.name, self.place, self.next, self.prev = name, place, following, previous
            self.source, self.mid_in, self.into = source, mid_in, into
            self.half, self.by_lanes = half, by_lanes

        def piece(self, ref, base, chunk, half, h):
            if self.by_lanes:
                return ref.at[rows_of(base + chunk * half, half), pl.ds(h * 256, 256)]
            return ref.at[rows_of(base + chunk * 2 * half + h * half, half), :]

        def begin(self, w, base, half, at):
            mid_at = at if self.by_lanes else at // 2
            mid_rows = pl.ds(mid_at, half)
            here = functools.partial(self.piece, self.source, base)
            far, up, down = (self.place + 2) % 4, (self.place + 1) % 4, (self.place + 3) % 4
            a_up = send(here(far, half, 0), self.mid_in.at[0, mid_rows], self.next)
            a_down = send(here(far, half, 1), self.mid_in.at[1, mid_rows], self.prev)
            b_up = send(here(up, half, 1), self.piece(self.into.at[0], at, 0, half, 1), self.next)
            b_down = send(here(down, half, 0), self.piece(self.into.at[1], at, 0, half, 0), self.prev)
            waiting[self.name, w] = (a_up, a_down, b_up, b_down)

        def middle(self, w, base, half, at):
            mid_at = at if self.by_lanes else at // 2
            a_up, a_down, b_up, b_down = waiting.pop((self.name, w))
            up, down = (self.place + 1) % 4, (self.place + 3) % 4
            sends = []
            for h, chunk, copy, device in ((0, up, a_up, self.next), (1, down, a_down, self.prev)):
                copy.wait_recv()
                if self.by_lanes:
                    rows, lanes = rows_of(base + chunk * half, half), pl.ds(h * 256, 256)
                    self.source[rows, lanes] = (
                        self.source[rows, lanes].astype(F32) + self.mid_in[h, pl.ds(mid_at, half)].astype(F32)
                    ).astype(BF16)
                else:
                    first = base + chunk * 2 * half + h * half
                    add_rows(self.source, first, ((self.source, first), (self.mid_in.at[h], mid_at)), half)
                sends.append(send(
                    self.piece(self.source, base, chunk, half, h), self.piece(self.into.at[h], at, 0, half, h), device
                ))
            waiting[self.name, w] = (b_up, b_down, *sends)

        def arrive(self, w):
            for copy in waiting.pop((self.name, w)):
                copy.wait_recv()

    x_axis = Axis("x", x, x_next, x_prev, summed, x_mid_in, x_in, None, False)
    z_axis = Axis("z", zh, z_next, z_prev, x_sum, z_mid_in, z_in, None, True)
    y_axis = Axis("y", y, y_next, y_prev, part, y_mid_in, y_in, None, False)

    def x_args(w):
        g = KV_WAVES[w]
        return KV_AT[w] * 256, 32 * g, KV_AT[w] * 64

    def z_args(w):
        g = KV_WAVES[w]
        return KV_AT[w] * 64, 16 * g, KV_AT[w] * 16

    def y_args(v):
        return 8 * Y_AT[v], Y_WAVES[v], 2 * Y_AT[v]

    def chunk_row(w, x_, zh_=None):
        g = KV_WAVES[w]
        row = KV_AT[w] * 512 + core * 256 * g + (x_ % 4) * 64 * g
        return row if zh_ is None else row + (zh_ % 4) * 16 * g

    def do_pair(w):
        waiting.pop(("pair", w)).wait_recv()
        at, size = own_rows(w, core)
        add_rows(summed, KV_AT[w] * 256, ((enc, at), (pair_in, KV_AT[w] * 256)), size)
        x_axis.begin(w, *x_args(w))

    def do_x_end(w):
        x_axis.arrive(w)
        base, half, at = x_args(w)
        add_rows(
            x_sum, at, ((summed, base + x * 2 * half), (x_in.at[0], at), (x_in.at[1], at)), 2 * half
        )
        z_axis.begin(w, *z_args(w))

    def do_z_end(w):
        z_axis.arrive(w)
        base, half, at = z_args(w)
        rows = pl.ds(at, half)
        total = (
            x_sum[rows_of(base + zh * half, half), :].astype(F32) + z_in[0, rows].astype(F32) + z_in[1, rows].astype(F32)
        )
        requant = (total * (1.0 / math.sqrt(32.0))).astype(BF16)
        row = chunk_row(w, x, zh)
        for j in range(4):
            lanes = slice(j * HEAD, (j + 1) * HEAD)
            decoded = jnp.dot(requant[:, lanes], hadamard.astype(BF16), preferred_element_type=F32)
            grad_out[rows_of(row, half), lanes] = (
                decoded * (1.0 / math.sqrt(HEAD)) * sign_row[:, lanes]
            ).astype(BF16)
        whole = grad_out.at[rows_of(row, half), :]
        waiting["zg", w] = (send(whole, whole, z_next), send(whole, whole, z_prev))

    def do_z_pass(w):
        up, down = waiting.pop(("zg", w))
        half = 16 * KV_WAVES[w]
        up.wait_recv()
        piece = grad_out.at[rows_of(chunk_row(w, x, zh + 3), half), pl.ds(0, 256)]
        first = send(piece, piece, z_next)
        down.wait_recv()
        piece = grad_out.at[rows_of(chunk_row(w, x, zh + 1), half), pl.ds(256, 256)]
        second = send(piece, piece, z_prev)
        waiting["zg", w] = (first, second)

    def do_x_own(w):
        for copy in waiting.pop(("zg", w)):
            copy.wait_recv()
        whole = grad_out.at[rows_of(chunk_row(w, x), 64 * KV_WAVES[w]), :]
        waiting["xg", w] = (send(whole, whole, x_next), send(whole, whole, x_prev))
        waiting["pg", w] = [send(whole, whole, peer)]

    def do_x_pass(w):
        up, down = waiting.pop(("xg", w))
        half = 32 * KV_WAVES[w]
        up.wait_recv()
        piece = grad_out.at[rows_of(chunk_row(w, x + 3), half), :]
        first = send(piece, piece, x_next)
        whole = grad_out.at[rows_of(chunk_row(w, x + 3), 2 * half), :]
        waiting["pg", w].append(send(whole, whole, peer))
        down.wait_recv()
        piece = grad_out.at[rows_of(chunk_row(w, x + 1) + half, half), :]
        second = send(piece, piece, x_prev)
        whole = grad_out.at[rows_of(chunk_row(w, x + 1), 2 * half), :]
        waiting["pg", w].append(send(whole, whole, peer))
        waiting["xg", w] = (first, second)

    def do_pair_last(w):
        for copy in waiting.pop(("xg", w)):
            copy.wait_recv()
        whole = grad_out.at[rows_of(chunk_row(w, x + 2), 64 * KV_WAVES[w]), :]
        waiting["pg", w].append(send(whole, whole, peer))

    def partial(v):
        for copy in weight_loads[v]:
            copy.wait()
        tile_rows = 512

        def tile(i, _):
            rows = rows_of(8 * Y_AT[v] + i * tile_rows, tile_rows)
            part[rows, :] = lax.dot_general(
                weight[rows, :], masked[...], (((1,), (1,)), ((), ())), preferred_element_type=F32
            ).astype(BF16)
            return 0

        lax.fori_loop(0, 8 * Y_WAVES[v] // tile_rows, tile, 0)

    def do_y_end(v):
        y_axis.arrive(v)
        base, half, at = y_args(v)
        add_rows(y_sum, at, ((part, base + y * 2 * half), (y_in.at[0], at), (y_in.at[1], at)), 2 * half)
        waiting["zl", v] = send(
            y_sum.at[rows_of(at + (1 - zl) * half, half), :], zl_in.at[pl.ds(Y_AT[v], half), :], zl_peer
        )

    def do_zl_end(v):
        waiting.pop(("zl", v)).wait_recv()
        base, half, at = y_args(v)
        total = (
            y_sum[rows_of(at + zl * half, half), :].astype(F32) + zl_in[pl.ds(Y_AT[v], half), :].astype(F32)
        ).astype(BF16)
        input_out[pl.ds(Y_AT[v], half), :] = total

    met = False
    for name, w in order():
        if name == "encode":
            encode(w)
            if not met:
                pl.semaphore_wait(barrier, len(neighbours))
                met = True
            pair_send(w)
        elif name == "pair":
            do_pair(w)
        elif name == "x_mid":
            x_axis.middle(w, *x_args(w))
        elif name == "x_end":
            do_x_end(w)
        elif name == "z_mid":
            z_axis.middle(w, *z_args(w))
        elif name == "z_end":
            do_z_end(w)
        elif name == "z_pass":
            do_z_pass(w)
        elif name == "x_own":
            do_x_own(w)
        elif name == "x_pass":
            do_x_pass(w)
        elif name == "pair_last":
            do_pair_last(w)
        elif name == "partial":
            partial(w)
            y_axis.begin(w, *y_args(w))
        elif name == "y_mid":
            y_axis.middle(w, *y_args(w))
        elif name == "y_end":
            do_y_end(w)
        elif name == "zl_end":
            do_zl_end(w)

    for w in range(len(KV_WAVES)):
        for copy in waiting.pop(("pg", w)):
            copy.wait_recv()
    for copy in sent:
        copy.wait_send()


def local(hidden_in, kv_weight, kv_cotangent, token_counts, block_signs, level_table, level_index):
    hbm = pl.BlockSpec(memory_space=pltpu.HBM)
    vmem = pl.BlockSpec(memory_space=pltpu.VMEM)
    grad, input_t = pl.pallas_call(
        kernel,
        out_shape=(
            jax.ShapeDtypeStruct((4608, 512), BF16),
            jax.ShapeDtypeStruct((576, 512), BF16),
        ),
        in_specs=[pl.BlockSpec(memory_space=pltpu.SMEM)] + [hbm] * 6,
        out_specs=(vmem, vmem),
        scratch_shapes=[
            pltpu.VMEM((512, 4608), BF16),
            pltpu.VMEM((4608, 512), BF16),
            pltpu.VMEM((512, 512), BF16),
            pltpu.VMEM((1, 512), jnp.int32),
            pltpu.VMEM((1, 256), F32),
            pltpu.VMEM((4, 4608), jnp.int32),
            pltpu.VMEM((512, 512), BF16),
            pltpu.VMEM((4608, 512), BF16),
            pltpu.VMEM((2304, 512), BF16),
            pltpu.VMEM((2304, 512), BF16),
            pltpu.VMEM((2, 288, 512), BF16),
            pltpu.VMEM((2, 576, 512), BF16),
            pltpu.VMEM((576, 512), BF16),
            pltpu.VMEM((2, 144, 256), BF16),
            pltpu.VMEM((2, 144, 512), BF16),
            pltpu.VMEM((4608, 512), BF16),
            pltpu.VMEM((2, 576, 512), BF16),
            pltpu.VMEM((2, 1152, 512), BF16),
            pltpu.VMEM((1152, 512), BF16),
            pltpu.VMEM((576, 512), BF16),
            pltpu.SemaphoreType.DMA((64,)),
            pltpu.SemaphoreType.DMA((192,)),
            pltpu.SemaphoreType.DMA((192,)),
        ],
        compiler_params=pltpu.CompilerParams(
            collective_id=0, has_side_effects=True, vmem_limit_bytes=48 * 2**20
        ),
        cost_estimate=pl.CostEstimate(flops=5 * 10**9, bytes_accessed=15 * 10**6, transcendentals=0),
        name="reduce_both",
    )(
        token_counts, hidden_in, kv_weight, kv_cotangent, block_signs.reshape(1, 512), level_table.reshape(1, 256),
        level_index,
    )
    return input_t.T, grad


def solution(mesh):
    return jax.shard_map(
        local,
        mesh=mesh,
        in_specs=(
            P("dp", None),
            P(None, "tensor"),
            P("dp", "tensor"),
            P("dp"),
            P("tensor"),
            P(),
            P("tensor", None),
        ),
        out_specs=(P("dp", "tensor"), P(None, "tensor")),
        check_vma=False,
    )
```

```python
import functools
import math

import jax
import jax.numpy as jnp
from jax import lax
from jax.experimental import pallas as pl
from jax.experimental.pallas import tpu as pltpu
from jax.sharding import PartitionSpec as P

MESH = pl.DeviceIdType.MESH
F32 = jnp.float32
BF16 = jnp.bfloat16
HEAD = 128
NX, NZ, NY = 4, 4, 4

KV_WAVES = (1, 1, 1, 1, 1, 1, 1, 1, 1)
Y_WAVES = (64, 128, 128, 128, 128)


def starts(sizes):
    out, at = [], 0
    for size in sizes:
        out.append(at)
        at += size
    return tuple(out)


KV_AT = starts(KV_WAVES)
Y_AT = starts(Y_WAVES)


ORDER = (
    ("encode", 0), ("encode", 1), ("partial", 0), ("encode", 2), ("encode", 3), ("encode", 4), ("pair", 1),
    ("pair", 2), ("pair", 3), ("encode", 5), ("encode", 6), ("encode", 7), ("x_mid", 1), ("y_mid", 0),
    ("x_mid", 2), ("pair", 0), ("pair", 5), ("partial", 1), ("x_end", 1), ("x_mid", 3), ("partial", 2),
    ("x_end", 2), ("pair", 7), ("encode", 8), ("y_end", 0), ("x_mid", 5), ("x_mid", 0), ("partial", 3),
    ("z_mid", 1), ("x_mid", 7), ("z_mid", 2), ("x_end", 3), ("pair", 8), ("pair", 4), ("x_end", 5),
    ("x_end", 0), ("z_end", 1), ("x_end", 7), ("z_end", 2), ("x_mid", 8), ("z_mid", 3), ("x_mid", 4),
    ("z_mid", 5), ("zl_end", 0), ("y_mid", 2), ("z_mid", 0), ("pair", 6), ("z_pass", 1), ("x_end", 8),
    ("z_mid", 7), ("x_end", 4), ("y_mid", 1), ("z_pass", 2), ("z_end", 3), ("x_mid", 6), ("z_end", 5),
    ("z_end", 0), ("z_mid", 8), ("y_mid", 3), ("z_mid", 4), ("x_own", 1), ("x_end", 6), ("z_pass", 3),
    ("z_end", 7), ("x_own", 2), ("z_pass", 5), ("z_pass", 0), ("z_end", 8), ("x_pass", 1), ("z_mid", 6),
    ("z_end", 4), ("x_own", 3), ("partial", 4), ("x_own", 5), ("z_pass", 7), ("z_pass", 8), ("x_pass", 2),
    ("z_end", 6), ("pair_last", 1), ("x_own", 0), ("z_pass", 4), ("y_end", 2), ("x_own", 7), ("x_own", 8),
    ("z_pass", 6), ("pair_last", 2), ("x_pass", 0), ("x_pass", 5), ("y_end", 3), ("y_end", 1), ("y_mid", 4),
    ("x_pass", 3), ("x_own", 4), ("x_own", 6), ("x_pass", 8), ("pair_last", 0), ("pair_last", 3), ("zl_end", 2),
    ("pair_last", 5), ("x_pass", 7), ("x_pass", 4), ("y_end", 4), ("x_pass", 6), ("pair_last", 7),
    ("pair_last", 4), ("pair_last", 8), ("pair_last", 6), ("zl_end", 1), ("zl_end", 3), ("zl_end", 4),
)


def rows_of(at, size):
    return pl.ds(pl.multiple_of(at, 16), size)


def add_rows(out, out_at, terms, size, block=32):
    block = min(block, size)

    def step(i, _):
        total = None
        for ref, at in terms:
            value = ref[rows_of(at + i * block, block), :].astype(F32)
            total = value if total is None else total + value
        out[rows_of(out_at + i * block, block), :] = total.astype(BF16)
        return 0

    lax.fori_loop(0, size // block, step, 0)


def kernel(
    count, hidden_hbm, weight_hbm, cot_hbm, signs_hbm, table_hbm, index_hbm,
    grad_out, input_out,
    hidden, weight, masked, signs, table, index, bt, enc, pair_in, summed,
    x_mid_in, x_in, x_sum, z_mid_in, z_in, part, y_mid_in, y_in, y_sum, zl_in,
    local_sem, send_sem, recv_sem,
):
    dp, tensor = lax.axis_index("dp"), lax.axis_index("tensor")
    zh, x, core = dp // 8, (dp // 2) % 4, dp % 2
    y, zl = tensor // 2, tensor % 2

    def dp_of(zh_, x_, core_):
        return ((zh_ % 4) * 4 + (x_ % 4)) * 2 + core_

    def at_dp(zh_, x_, core_):
        return (dp_of(zh_, x_, core_), tensor)

    peer = at_dp(zh, x, 1 - core)
    x_next, x_prev = at_dp(zh, x + 1, core), at_dp(zh, x + 3, core)
    z_next, z_prev = at_dp(zh + 1, x, core), at_dp(zh + 3, x, core)
    y_next, y_prev = (dp, ((y + 1) % 4) * 2 + zl), (dp, ((y + 3) % 4) * 2 + zl)
    zl_peer = (dp, y * 2 + 1 - zl)
    neighbours = (peer, x_next, x_prev, z_next, z_prev, y_next, y_prev, zl_peer)

    used = [0]
    local_used = [0]
    sent = []

    def load(src, dst):
        copy = pltpu.make_async_copy(src, dst, local_sem.at[local_used[0]])
        local_used[0] += 1
        copy.start()
        return copy

    def send(src, dst, device):
        copy = pltpu.make_async_remote_copy(
            src_ref=src, dst_ref=dst, send_sem=send_sem.at[used[0]], recv_sem=recv_sem.at[used[0]],
            device_id=device, device_id_type=MESH,
        )
        used[0] += 1
        copy.start()
        sent.append(copy)
        return copy

    cot_load = load(cot_hbm, masked)
    small_loads = [load(signs_hbm, signs), load(table_hbm, table), load(index_hbm, index)]
    hidden_loads, weight_loads = [], []

    def load_hidden(first, last):
        lanes = pl.ds(KV_AT[first] * 512, sum(KV_WAVES[first:last]) * 512)
        copy = load(hidden_hbm.at[:, lanes], hidden.at[:, lanes])
        hidden_loads.extend([copy] + [None] * (last - first - 1))

    def load_weight(v):
        rows = pl.ds(Y_AT[v], Y_WAVES[v])
        weight_loads.append(load(weight_hbm.at[:, rows, :], weight.at[:, rows, :]))

    load_hidden(0, 1)
    barrier = pltpu.get_barrier_semaphore()
    for device in neighbours:
        pl.semaphore_signal(barrier, inc=1, device_id=device, device_id_type=MESH)


    def load_rest():
        load_weight(0)
        for w in range(1, len(KV_WAVES), 2):
            load_hidden(w, min(w + 2, len(KV_WAVES)))
            if len(weight_loads) < len(Y_WAVES):
                load_weight(len(weight_loads))
        while len(weight_loads) < len(Y_WAVES):
            load_weight(len(weight_loads))

    row_i = lax.broadcasted_iota(jnp.int32, (HEAD, HEAD), 0)
    col_i = lax.broadcasted_iota(jnp.int32, (HEAD, HEAD), 1)
    common = row_i & col_i
    common = common ^ (common >> 4)
    common = common ^ (common >> 2)
    common = common ^ (common >> 1)
    hadamard = (1 - 2 * (common & 1)).astype(F32)

    cot_load.wait()
    tokens = lax.broadcasted_iota(jnp.int32, (512, 512), 0)
    masked[...] = jnp.where(tokens < count[0], masked[...].astype(F32), 0.0).astype(BF16)
    for copy in small_loads:
        copy.wait()
    sign_row = (2 * signs[...] - 1).astype(F32)
    for j in range(4):
        lanes = pl.ds(j * HEAD, HEAD)
        turned = (hadamard * sign_row[:, j * HEAD:(j + 1) * HEAD]).astype(BF16)
        bt[lanes, :] = (
            lax.dot_general(turned, masked[:, lanes], (((1,), (1,)), ((), ())), preferred_element_type=F32)
            * (1.0 / 256.0)
        ).astype(BF16)

    waiting = {}

    def encode(w):
        if hidden_loads[w] is not None:
            hidden_loads[w].wait()

        def tile(i, _):
            at = pl.multiple_of((KV_AT[w] + i) * 512, 512)
            value = jnp.dot(bt[...], hidden[:, pl.ds(at, 512)], preferred_element_type=F32)
            low = jnp.broadcast_to(table[:, 0:128], (4, 128))
            high = jnp.broadcast_to(table[:, 128:256], (4, 128))
            bounds = []
            for k in range(4):
                ids = index[:, pl.ds(at + k * 128, 128)]
                first = jnp.take_along_axis(low, ids & 127, axis=1, mode="promise_in_bounds")
                second = jnp.take_along_axis(high, ids & 127, axis=1, mode="promise_in_bounds")
                bounds.append(jnp.where(ids >= 128, second, first))
            bound = jnp.concatenate(bounds, axis=1)
            for j in range(4):
                limit = bound[j:j + 1, :]
                clipped = jnp.clip(value[j * HEAD:(j + 1) * HEAD], -limit, limit).astype(BF16)
                enc[pl.ds(at, 512), pl.ds(j * HEAD, HEAD)] = clipped.T
            return 0

        lax.fori_loop(0, KV_WAVES[w], tile, 0)

    def own_rows(w, core_):
        g = KV_WAVES[w]
        return KV_AT[w] * 512 + core_ * 256 * g, 256 * g

    def pair_send(w):
        at, size = own_rows(w, 1 - core)
        waiting["pair", w] = send(
            enc.at[rows_of(at, size), :], pair_in.at[pl.ds(KV_AT[w] * 256, size), :], peer
        )

    class Axis:
        def __init__(self, name, place, following, previous, source, mid_in, into, half, by_lanes):
            self.name, self.place, self.next, self.prev = name, place, following, previous
            self.source, self.mid_in, self.into = source, mid_in, into
            self.half, self.by_lanes = half, by_lanes

        def piece(self, ref, base, chunk, half, h):
            if self.by_lanes:
                return ref.at[rows_of(base + chunk * half, half), pl.ds(h * 256, 256)]
            return ref.at[rows_of(base + chunk * 2 * half + h * half, half), :]

        def begin(self, w, base, half, at):
            mid_at = at if self.by_lanes else at // 2
            mid_rows = pl.ds(mid_at, half)
            here = functools.partial(self.piece, self.source, base)
            far, up, down = (self.place + 2) % 4, (self.place + 1) % 4, (self.place + 3) % 4
            a_up = send(here(far, half, 0), self.mid_in.at[0, mid_rows], self.next)
            a_down = send(here(far, half, 1), self.mid_in.at[1, mid_rows], self.prev)
            b_up = send(here(up, half, 1), self.piece(self.into.at[0], at, 0, half, 1), self.next)
            b_down = send(here(down, half, 0), self.piece(self.into.at[1], at, 0, half, 0), self.prev)
            waiting[self.name, w] = (a_up, a_down, b_up, b_down)

        def middle(self, w, base, half, at):
            mid_at = at if self.by_lanes else at // 2
            a_up, a_down, b_up, b_down = waiting.pop((self.name, w))
            up, down = (self.place + 1) % 4, (self.place + 3) % 4
            sends = []
            for h, chunk, copy, device in ((0, up, a_up, self.next), (1, down, a_down, self.prev)):
                copy.wait_recv()
                if self.by_lanes:
                    rows, lanes = rows_of(base + chunk * half, half), pl.ds(h * 256, 256)
                    self.source[rows, lanes] = (
                        self.source[rows, lanes].astype(F32) + self.mid_in[h, pl.ds(mid_at, half)].astype(F32)
                    ).astype(BF16)
                else:
                    first = base + chunk * 2 * half + h * half
                    add_rows(self.source, first, ((self.source, first), (self.mid_in.at[h], mid_at)), half)
                sends.append(send(
                    self.piece(self.source, base, chunk, half, h), self.piece(self.into.at[h], at, 0, half, h), device
                ))
            waiting[self.name, w] = (b_up, b_down, *sends)

        def arrive(self, w):
            for copy in waiting.pop((self.name, w)):
                copy.wait_recv()

    x_axis = Axis("x", x, x_next, x_prev, summed, x_mid_in, x_in, None, False)
    z_axis = Axis("z", zh, z_next, z_prev, x_sum, z_mid_in, z_in, None, True)
    y_axis = Axis("y", y, y_next, y_prev, part, y_mid_in, y_in, None, False)

    def x_args(w):
        g = KV_WAVES[w]
        return KV_AT[w] * 256, 32 * g, KV_AT[w] * 64

    def z_args(w):
        g = KV_WAVES[w]
        return KV_AT[w] * 64, 16 * g, KV_AT[w] * 16

    def y_args(v):
        return 8 * Y_AT[v], Y_WAVES[v], 2 * Y_AT[v]

    def chunk_row(w, x_, zh_=None):
        g = KV_WAVES[w]
        row = KV_AT[w] * 512 + core * 256 * g + (x_ % 4) * 64 * g
        return row if zh_ is None else row + (zh_ % 4) * 16 * g

    def do_pair(w):
        waiting.pop(("pair", w)).wait_recv()
        at, size = own_rows(w, core)
        add_rows(summed, KV_AT[w] * 256, ((enc, at), (pair_in, KV_AT[w] * 256)), size)
        x_axis.begin(w, *x_args(w))

    def do_x_end(w):
        x_axis.arrive(w)
        base, half, at = x_args(w)
        add_rows(
            x_sum, at, ((summed, base + x * 2 * half), (x_in.at[0], at), (x_in.at[1], at)), 2 * half
        )
        z_axis.begin(w, *z_args(w))

    def do_z_end(w):
        z_axis.arrive(w)
        base, half, at = z_args(w)
        rows = pl.ds(at, half)
        total = (
            x_sum[rows_of(base + zh * half, half), :].astype(F32) + z_in[0, rows].astype(F32) + z_in[1, rows].astype(F32)
        )
        requant = (total * (1.0 / math.sqrt(32.0))).astype(BF16)
        row = chunk_row(w, x, zh)
        for j in range(4):
            lanes = slice(j * HEAD, (j + 1) * HEAD)
            decoded = jnp.dot(requant[:, lanes], hadamard.astype(BF16), preferred_element_type=F32)
            grad_out[rows_of(row, half), lanes] = (
                decoded * (1.0 / math.sqrt(HEAD)) * sign_row[:, lanes]
            ).astype(BF16)
        whole = grad_out.at[rows_of(row, half), :]
        waiting["zg", w] = (send(whole, whole, z_next), send(whole, whole, z_prev))

    def do_z_pass(w):
        up, down = waiting.pop(("zg", w))
        half = 16 * KV_WAVES[w]
        up.wait_recv()
        piece = grad_out.at[rows_of(chunk_row(w, x, zh + 3), half), pl.ds(0, 256)]
        first = send(piece, piece, z_next)
        down.wait_recv()
        piece = grad_out.at[rows_of(chunk_row(w, x, zh + 1), half), pl.ds(256, 256)]
        second = send(piece, piece, z_prev)
        waiting["zg", w] = (first, second)

    def do_x_own(w):
        for copy in waiting.pop(("zg", w)):
            copy.wait_recv()
        whole = grad_out.at[rows_of(chunk_row(w, x), 64 * KV_WAVES[w]), :]
        waiting["xg", w] = (send(whole, whole, x_next), send(whole, whole, x_prev))
        waiting["pg", w] = [send(whole, whole, peer)]

    def do_x_pass(w):
        up, down = waiting.pop(("xg", w))
        half = 32 * KV_WAVES[w]
        up.wait_recv()
        piece = grad_out.at[rows_of(chunk_row(w, x + 3), half), :]
        first = send(piece, piece, x_next)
        whole = grad_out.at[rows_of(chunk_row(w, x + 3), 2 * half), :]
        waiting["pg", w].append(send(whole, whole, peer))
        down.wait_recv()
        piece = grad_out.at[rows_of(chunk_row(w, x + 1) + half, half), :]
        second = send(piece, piece, x_prev)
        whole = grad_out.at[rows_of(chunk_row(w, x + 1), 2 * half), :]
        waiting["pg", w].append(send(whole, whole, peer))
        waiting["xg", w] = (first, second)

    def do_pair_last(w):
        for copy in waiting.pop(("xg", w)):
            copy.wait_recv()
        whole = grad_out.at[rows_of(chunk_row(w, x + 2), 64 * KV_WAVES[w]), :]
        waiting["pg", w].append(send(whole, whole, peer))

    def partial(v):
        weight_loads[v].wait()
        size = Y_WAVES[v]

        def tile(i, _):
            rows = weight[pl.ds(i * 4, 4), pl.ds(Y_AT[v], size), :].reshape(4 * size, 512)
            part[rows_of(8 * Y_AT[v] + i * 4 * size, 4 * size), :] = lax.dot_general(
                rows, masked[...], (((1,), (1,)), ((), ())), preferred_element_type=F32
            ).astype(BF16)
            return 0

        lax.fori_loop(0, 2, tile, 0)

    def do_y_end(v):
        y_axis.arrive(v)
        base, half, at = y_args(v)
        add_rows(y_sum, at, ((part, base + y * 2 * half), (y_in.at[0], at), (y_in.at[1], at)), 2 * half)
        waiting["zl", v] = send(
            y_sum.at[rows_of(at + (1 - zl) * half, half), :], zl_in.at[pl.ds(Y_AT[v], half), :], zl_peer
        )

    def do_zl_end(v):
        waiting.pop(("zl", v)).wait_recv()
        base, half, at = y_args(v)
        total = (
            y_sum[rows_of(at + zl * half, half), :].astype(F32) + zl_in[pl.ds(Y_AT[v], half), :].astype(F32)
        ).astype(BF16)
        input_out[pl.ds(Y_AT[v], half), :] = total

    met = False
    for name, w in ORDER:
        if name == "encode":
            encode(w)
            if not met:
                pl.semaphore_wait(barrier, len(neighbours))
            pair_send(w)
            if not met:
                load_rest()
                met = True
        elif name == "pair":
            do_pair(w)
        elif name == "x_mid":
            x_axis.middle(w, *x_args(w))
        elif name == "x_end":
            do_x_end(w)
        elif name == "z_mid":
            z_axis.middle(w, *z_args(w))
        elif name == "z_end":
            do_z_end(w)
        elif name == "z_pass":
            do_z_pass(w)
        elif name == "x_own":
            do_x_own(w)
        elif name == "x_pass":
            do_x_pass(w)
        elif name == "pair_last":
            do_pair_last(w)
        elif name == "partial":
            partial(w)
            y_axis.begin(w, *y_args(w))
        elif name == "y_mid":
            y_axis.middle(w, *y_args(w))
        elif name == "y_end":
            do_y_end(w)
        elif name == "zl_end":
            do_zl_end(w)

    for w in range(len(KV_WAVES)):
        for copy in waiting.pop(("pg", w)):
            copy.wait_recv()
    for copy in sent:
        copy.wait_send()


def local(hidden_in, kv_weight, kv_cotangent, token_counts, block_signs, level_table, level_index):
    hbm = pl.BlockSpec(memory_space=pltpu.HBM)
    vmem = pl.BlockSpec(memory_space=pltpu.VMEM)
    grad, input_t = pl.pallas_call(
        kernel,
        out_shape=(
            jax.ShapeDtypeStruct((4608, 512), BF16),
            jax.ShapeDtypeStruct((576, 512), BF16),
        ),
        in_specs=[pl.BlockSpec(memory_space=pltpu.SMEM)] + [hbm] * 6,
        out_specs=(vmem, vmem),
        scratch_shapes=[
            pltpu.VMEM((512, 4608), BF16),
            pltpu.VMEM((8, 576, 512), BF16),
            pltpu.VMEM((512, 512), BF16),
            pltpu.VMEM((1, 512), jnp.int32),
            pltpu.VMEM((1, 256), F32),
            pltpu.VMEM((4, 4608), jnp.int32),
            pltpu.VMEM((512, 512), BF16),
            pltpu.VMEM((4608, 512), BF16),
            pltpu.VMEM((2304, 512), BF16),
            pltpu.VMEM((2304, 512), BF16),
            pltpu.VMEM((2, 288, 512), BF16),
            pltpu.VMEM((2, 576, 512), BF16),
            pltpu.VMEM((576, 512), BF16),
            pltpu.VMEM((2, 144, 256), BF16),
            pltpu.VMEM((2, 144, 512), BF16),
            pltpu.VMEM((4608, 512), BF16),
            pltpu.VMEM((2, 576, 512), BF16),
            pltpu.VMEM((2, 1152, 512), BF16),
            pltpu.VMEM((1152, 512), BF16),
            pltpu.VMEM((576, 512), BF16),
            pltpu.SemaphoreType.DMA((64,)),
            pltpu.SemaphoreType.DMA((288,)),
            pltpu.SemaphoreType.DMA((288,)),
        ],
        compiler_params=pltpu.CompilerParams(
            collective_id=0, has_side_effects=True, vmem_limit_bytes=48 * 2**20
        ),
        cost_estimate=pl.CostEstimate(flops=5 * 10**9, bytes_accessed=15 * 10**6, transcendentals=0),
        name="reduce_both",
    )(token_counts, *(
        pltpu.with_memory_space_constraint(array, pltpu.HBM)
        for array in (
            hidden_in, kv_weight.reshape(8, 576, 512), kv_cotangent, block_signs.reshape(1, 512),
            level_table.reshape(1, 256), level_index,
        )
    ))
    return input_t.T, grad


def solution(mesh):
    return jax.shard_map(
        local,
        mesh=mesh,
        in_specs=(
            P("dp", None),
            P(None, "tensor"),
            P("dp", "tensor"),
            P("dp"),
            P("tensor"),
            P(),
            P("tensor", None),
        ),
        out_specs=(P("dp", "tensor"), P(None, "tensor")),
        check_vma=False,
    )
```

```python
import functools
import math

import jax
import jax.numpy as jnp
from jax import lax
from jax.experimental import pallas as pl
from jax.experimental.pallas import tpu as pltpu
from jax.sharding import PartitionSpec as P

MESH = pl.DeviceIdType.MESH
SEND_SLOTS = 16
F32 = jnp.float32
BF16 = jnp.bfloat16
HEAD = 128
NX, NZ, NY = 4, 4, 4

KV_WAVES = (1, 1, 1, 1, 1, 1, 1, 1, 1)
Y_WAVES = (64, 128, 128, 128, 128)


def starts(sizes):
    out, at = [], 0
    for size in sizes:
        out.append(at)
        at += size
    return tuple(out)


KV_AT = starts(KV_WAVES)
Y_AT = starts(Y_WAVES)


ORDER = (
    ("encode", 0), ("partial", 0), ("encode", 1), ("encode", 2), ("pair", 0), ("encode", 3), ("pair", 1),
    ("encode", 4), ("pair", 2), ("partial", 1), ("encode", 5), ("x_mid", 0), ("encode", 6), ("pair", 4),
    ("encode", 7), ("x_mid", 1), ("x_mid", 2), ("pair", 3), ("partial", 4), ("x_end", 0), ("x_mid", 4),
    ("partial", 2), ("pair", 5), ("x_end", 1), ("encode", 8), ("x_end", 2), ("x_mid", 3), ("pair", 6),
    ("pair", 7), ("x_end", 4), ("z_end", 0), ("pair", 8), ("x_end", 3), ("x_mid", 6), ("z_end", 1),
    ("partial", 3), ("z_end", 2), ("y_mid", 0), ("x_mid", 5), ("z_end", 4), ("x_mid", 8), ("y_mid", 1),
    ("y_mid", 2), ("x_end", 6), ("x_mid", 7), ("x_own", 0), ("x_end", 5), ("x_end", 8), ("x_own", 1),
    ("x_end", 7), ("x_own", 2), ("z_end", 3), ("x_own", 4), ("z_end", 6), ("z_end", 5), ("x_pass", 2),
    ("z_end", 8), ("x_pass", 0), ("x_pass", 4), ("y_mid", 3), ("x_pass", 1), ("z_end", 7), ("y_end", 1),
    ("x_own", 3), ("y_mid", 4), ("x_own", 6), ("y_end", 2), ("x_own", 5), ("x_own", 8), ("y_end", 3),
    ("y_end", 0), ("x_own", 7), ("x_pass", 3), ("y_end", 4), ("zl_end", 1), ("pair_last", 0), ("pair_last", 2),
    ("x_pass", 5), ("x_pass", 6), ("x_pass", 8), ("pair_last", 4), ("pair_last", 1), ("x_pass", 7),
    ("pair_last", 3), ("pair_last", 5), ("pair_last", 6), ("pair_last", 8), ("zl_end", 3), ("pair_last", 7),
    ("zl_end", 0), ("zl_end", 2), ("zl_end", 4),
)


def rows_of(at, size):
    return pl.ds(pl.multiple_of(at, 16), size)


def add_rows(out, out_at, terms, size, block=32):
    block = min(block, size)

    def step(i, _):
        total = None
        for ref, at in terms:
            value = ref[rows_of(at + i * block, block), :].astype(F32)
            total = value if total is None else total + value
        out[rows_of(out_at + i * block, block), :] = total.astype(BF16)
        return 0

    lax.fori_loop(0, size // block, step, 0)


def kernel(
    count, hidden_hbm, weight_hbm, cot_hbm, signs_hbm, table_hbm, index_hbm,
    grad_out, input_out,
    hidden, weight, masked, signs, table, index, bt, enc, pair_in, summed,
    x_mid_in, x_in, x_sum, z_in, part, y_mid_in, y_in, y_sum, zl_in,
    local_sem, send_sem, recv_sem,
):
    dp, tensor = lax.axis_index("dp"), lax.axis_index("tensor")
    zh, x, core = dp // 8, (dp // 2) % 4, dp % 2
    y, zl = tensor // 2, tensor % 2

    def dp_of(zh_, x_, core_):
        return ((zh_ % 4) * 4 + (x_ % 4)) * 2 + core_

    def at_dp(zh_, x_, core_):
        return (dp_of(zh_, x_, core_), tensor)

    peer = at_dp(zh, x, 1 - core)
    x_next, x_prev = at_dp(zh, x + 1, core), at_dp(zh, x + 3, core)
    z_next, z_prev, z_far = at_dp(zh + 1, x, core), at_dp(zh + 3, x, core), at_dp(zh + 2, x, core)
    z_others = ((zh + 1, z_next), (zh + 3, z_prev), (zh + 2, z_far))
    y_next, y_prev = (dp, ((y + 1) % 4) * 2 + zl), (dp, ((y + 3) % 4) * 2 + zl)
    zl_peer = (dp, y * 2 + 1 - zl)
    neighbours = (peer, x_next, x_prev, z_next, z_prev, z_far, y_next, y_prev, zl_peer)

    local_used = [0]
    arrivals = {}
    slots = [0] * SEND_SLOTS
    slot = [0]

    def drain(semaphore, rows):
        view = enc.at[pl.ds(0, rows), :]
        pltpu.make_async_copy(view, view, semaphore).wait()

    def wait_for(key):
        index, rows = arrivals.pop(key)
        drain(recv_sem.at[index], rows)

    recv_of = {}

    def next_slot():
        slot[0] = (slot[0] + 1) % SEND_SLOTS
        if slots[slot[0]]:
            drain(send_sem.at[slot[0]], slots[slot[0]])
            slots[slot[0]] = 0

    def load(src, dst):
        copy = pltpu.make_async_copy(src, dst, local_sem.at[local_used[0]])
        local_used[0] += 1
        copy.start()
        return copy

    def send(src, dst, device, key):
        index = recv_of.setdefault(key, len(recv_of))
        rows = src.shape[0] * src.shape[1] // 512
        copy = pltpu.make_async_remote_copy(
            src_ref=src, dst_ref=dst, send_sem=send_sem.at[slot[0]], recv_sem=recv_sem.at[index],
            device_id=device, device_id_type=MESH,
        )
        copy.start()
        slots[slot[0]] += rows
        arrivals[key] = [index, arrivals.get(key, (0, 0))[1] + rows]

    cot_load = load(cot_hbm, masked)
    barrier = pltpu.get_barrier_semaphore()
    for device in neighbours:
        pl.semaphore_signal(barrier, inc=1, device_id=device, device_id_type=MESH)
    small_loads = [load(signs_hbm, signs), load(table_hbm, table), load(index_hbm, index)]
    hidden_loads, weight_loads = [], []

    def load_hidden(first, last):
        lanes = pl.ds(KV_AT[first] * 512, sum(KV_WAVES[first:last]) * 512)
        copy = load(hidden_hbm.at[:, lanes], hidden.at[:, lanes])
        hidden_loads.extend([copy] + [None] * (last - first - 1))

    def load_weight(v):
        rows = pl.ds(Y_AT[v], Y_WAVES[v])
        weight_loads.append(load(weight_hbm.at[:, rows, :], weight.at[:, rows, :]))

    load_hidden(0, 1)
    def load_rest():
        load_weight(0)
        for w in range(1, len(KV_WAVES), 2):
            load_hidden(w, min(w + 2, len(KV_WAVES)))
            if len(weight_loads) < len(Y_WAVES):
                load_weight(len(weight_loads))
        while len(weight_loads) < len(Y_WAVES):
            load_weight(len(weight_loads))

    row_i = lax.broadcasted_iota(jnp.int32, (HEAD, HEAD), 0)
    col_i = lax.broadcasted_iota(jnp.int32, (HEAD, HEAD), 1)
    common = row_i & col_i
    common = common ^ (common >> 4)
    common = common ^ (common >> 2)
    common = common ^ (common >> 1)
    hadamard = (1 - 2 * (common & 1)).astype(F32)

    cot_load.wait()
    tokens = lax.broadcasted_iota(jnp.int32, (512, 512), 0)
    masked[...] = jnp.where(tokens < count[0], masked[...].astype(F32), 0.0).astype(BF16)
    for copy in small_loads:
        copy.wait()
    sign_row = (2 * signs[...] - 1).astype(F32)
    for j in range(4):
        lanes = pl.ds(j * HEAD, HEAD)
        turned = (hadamard * sign_row[:, j * HEAD:(j + 1) * HEAD]).astype(BF16)
        bt[lanes, :] = (
            lax.dot_general(turned, masked[:, lanes], (((1,), (1,)), ((), ())), preferred_element_type=F32)
            * (1.0 / 256.0)
        ).astype(BF16)

    def encode(w):
        if hidden_loads[w] is not None:
            hidden_loads[w].wait()

        def tile(i, _):
            at = pl.multiple_of((KV_AT[w] + i) * 512, 512)
            value = jnp.dot(bt[...], hidden[:, pl.ds(at, 512)], preferred_element_type=F32)
            low = jnp.broadcast_to(table[:, 0:128], (4, 128))
            high = jnp.broadcast_to(table[:, 128:256], (4, 128))
            bounds = []
            for k in range(4):
                ids = index[:, pl.ds(at + k * 128, 128)]
                first = jnp.take_along_axis(low, ids & 127, axis=1, mode="promise_in_bounds")
                second = jnp.take_along_axis(high, ids & 127, axis=1, mode="promise_in_bounds")
                bounds.append(jnp.where(ids >= 128, second, first))
            bound = jnp.concatenate(bounds, axis=1)
            for j in range(4):
                limit = bound[j:j + 1, :]
                clipped = jnp.clip(value[j * HEAD:(j + 1) * HEAD], -limit, limit).astype(BF16)
                enc[pl.ds(at, 512), pl.ds(j * HEAD, HEAD)] = clipped.T
            return 0

        lax.fori_loop(0, KV_WAVES[w], tile, 0)

    def own_rows(w, core_):
        g = KV_WAVES[w]
        return KV_AT[w] * 512 + core_ * 256 * g, 256 * g

    def pair_send(w):
        at, size = own_rows(w, 1 - core)
        send(enc.at[rows_of(at, size), :], pair_in.at[pl.ds(KV_AT[w] * 256, size), :], peer, ("pair", w))

    class Axis:
        def __init__(self, name, place, following, previous, source, mid_in, into):
            self.name, self.place, self.next, self.prev = name, place, following, previous
            self.source, self.mid_in, self.into = source, mid_in, into

        def piece(self, ref, base, chunk, half, h):
            return ref.at[rows_of(base + chunk * 2 * half + h * half, half), :]

        def begin(self, w, base, half, at):
            mid_rows = pl.ds(at // 2, half)
            here = functools.partial(self.piece, self.source, base)
            far, up, down = (self.place + 2) % 4, (self.place + 1) % 4, (self.place + 3) % 4
            send(here(far, half, 0), self.mid_in.at[0, mid_rows], self.next, (self.name, "mid", w))
            send(here(far, half, 1), self.mid_in.at[1, mid_rows], self.prev, (self.name, "mid", w))
            send(here(up, half, 1), self.piece(self.into.at[0], at, 0, half, 1), self.next, (self.name, "end", w))
            send(here(down, half, 0), self.piece(self.into.at[1], at, 0, half, 0), self.prev, (self.name, "end", w))

        def middle(self, w, base, half, at):
            up, down = (self.place + 1) % 4, (self.place + 3) % 4
            wait_for((self.name, "mid", w))
            for h, chunk, device in ((0, up, self.next), (1, down, self.prev)):
                first = base + chunk * 2 * half + h * half
                add_rows(self.source, first, ((self.source, first), (self.mid_in.at[h], at // 2)), half)
                send(
                    self.piece(self.source, base, chunk, half, h), self.piece(self.into.at[h], at, 0, half, h), device,
                    (self.name, "end", w),
                )

        def arrive(self, w):
            wait_for((self.name, "end", w))

    x_axis = Axis("x", x, x_next, x_prev, summed, x_mid_in, x_in)
    y_axis = Axis("y", y, y_next, y_prev, part, y_mid_in, y_in)

    def x_args(w):
        g = KV_WAVES[w]
        return KV_AT[w] * 256, 32 * g, KV_AT[w] * 64

    def z_args(w):
        g = KV_WAVES[w]
        return KV_AT[w] * 64, 16 * g

    def y_args(v):
        return 8 * Y_AT[v], Y_WAVES[v], 2 * Y_AT[v]

    def chunk_row(w, x_, zh_=None):
        g = KV_WAVES[w]
        row = KV_AT[w] * 512 + core * 256 * g + (x_ % 4) * 64 * g
        return row if zh_ is None else row + (zh_ % 4) * 16 * g

    def do_pair(w):
        wait_for(("pair", w))
        at, size = own_rows(w, core)
        add_rows(summed, KV_AT[w] * 256, ((enc, at), (pair_in, KV_AT[w] * 256)), size)
        x_axis.begin(w, *x_args(w))

    def do_x_end(w):
        x_axis.arrive(w)
        base, half, at = x_args(w)
        add_rows(
            x_sum, at, ((summed, base + x * 2 * half), (x_in.at[0], at), (x_in.at[1], at)), 2 * half
        )
        base, size = z_args(w)
        for i, (place, device) in enumerate(z_others):
            send(
                x_sum.at[rows_of(base + (place % 4) * size, size), :], z_in.at[i, pl.ds(KV_AT[w] * 16, size), :], device,
                ("z_end", w),
            )

    def do_z_end(w):
        wait_for(("z_end", w))
        base, half = z_args(w)
        rows = pl.ds(KV_AT[w] * 16, half)
        total = x_sum[rows_of(base + zh * half, half), :].astype(F32)
        for i in range(3):
            total = total + z_in[i, rows].astype(F32)
        requant = (total * (1.0 / math.sqrt(32.0))).astype(BF16)
        row = chunk_row(w, x, zh)
        for j in range(4):
            lanes = slice(j * HEAD, (j + 1) * HEAD)
            decoded = jnp.dot(requant[:, lanes], hadamard.astype(BF16), preferred_element_type=F32)
            grad_out[rows_of(row, half), lanes] = (
                decoded * (1.0 / math.sqrt(HEAD)) * sign_row[:, lanes]
            ).astype(BF16)
        whole = grad_out.at[rows_of(row, half), :]
        for _, device in z_others:
            send(whole, whole, device, ("z_own", w))

    def do_x_own(w):
        wait_for(("z_own", w))
        whole = grad_out.at[rows_of(chunk_row(w, x), 64 * KV_WAVES[w]), :]
        send(whole, whole, x_next, ("x_own", w))
        send(whole, whole, x_prev, ("x_own", w))
        send(whole, whole, peer, "last")

    def do_x_pass(w):
        half = 32 * KV_WAVES[w]
        wait_for(("x_own", w))
        for place, device, first in ((x + 3, x_next, 0), (x + 1, x_prev, half)):
            piece = grad_out.at[rows_of(chunk_row(w, place) + first, half), :]
            send(piece, piece, device, ("x_pass", w))
        for place in (x + 3, x + 1):
            whole = grad_out.at[rows_of(chunk_row(w, place), 2 * half), :]
            send(whole, whole, peer, "last")

    def do_pair_last(w):
        wait_for(("x_pass", w))
        whole = grad_out.at[rows_of(chunk_row(w, x + 2), 64 * KV_WAVES[w]), :]
        send(whole, whole, peer, "last")

    def partial(v):
        weight_loads[v].wait()
        size = Y_WAVES[v]

        def tile(i, _):
            rows = weight[pl.ds(i * 4, 4), pl.ds(Y_AT[v], size), :].reshape(4 * size, 512)
            part[rows_of(8 * Y_AT[v] + i * 4 * size, 4 * size), :] = lax.dot_general(
                rows, masked[...], (((1,), (1,)), ((), ())), preferred_element_type=F32
            ).astype(BF16)
            return 0

        lax.fori_loop(0, 2, tile, 0)

    def do_y_end(v):
        y_axis.arrive(v)
        base, half, at = y_args(v)
        add_rows(y_sum, at, ((part, base + y * 2 * half), (y_in.at[0], at), (y_in.at[1], at)), 2 * half)
        send(y_sum.at[rows_of(at + (1 - zl) * half, half), :], zl_in.at[pl.ds(Y_AT[v], half), :], zl_peer, ("zl", v))

    def do_zl_end(v):
        wait_for(("zl", v))
        base, half, at = y_args(v)
        total = (
            y_sum[rows_of(at + zl * half, half), :].astype(F32) + zl_in[pl.ds(Y_AT[v], half), :].astype(F32)
        ).astype(BF16)
        input_out[pl.ds(Y_AT[v], half), :] = total

    met = False
    for name, w in ORDER:
        next_slot()
        if name == "encode":
            encode(w)
            if not met:
                pl.semaphore_wait(barrier, len(neighbours))
            pair_send(w)
            if not met:
                load_rest()
                met = True
        elif name == "pair":
            do_pair(w)
        elif name == "x_mid":
            x_axis.middle(w, *x_args(w))
        elif name == "x_end":
            do_x_end(w)
        elif name == "z_end":
            do_z_end(w)
        elif name == "x_own":
            do_x_own(w)
        elif name == "x_pass":
            do_x_pass(w)
        elif name == "pair_last":
            do_pair_last(w)
        elif name == "partial":
            partial(w)
            y_axis.begin(w, *y_args(w))
        elif name == "y_mid":
            y_axis.middle(w, *y_args(w))
        elif name == "y_end":
            do_y_end(w)
        elif name == "zl_end":
            do_zl_end(w)

    wait_for("last")
    for index, rows in enumerate(slots):
        if rows:
            drain(send_sem.at[index], rows)


def local(hidden_in, kv_weight, kv_cotangent, token_counts, block_signs, level_table, level_index):
    hbm = pl.BlockSpec(memory_space=pltpu.HBM)
    vmem = pl.BlockSpec(memory_space=pltpu.VMEM)
    grad, input_t = pl.pallas_call(
        kernel,
        out_shape=(
            jax.ShapeDtypeStruct((4608, 512), BF16),
            jax.ShapeDtypeStruct((576, 512), BF16),
        ),
        in_specs=[pl.BlockSpec(memory_space=pltpu.SMEM)] + [hbm] * 6,
        out_specs=(vmem, vmem),
        scratch_shapes=[
            pltpu.VMEM((512, 4608), BF16),
            pltpu.VMEM((8, 576, 512), BF16),
            pltpu.VMEM((512, 512), BF16),
            pltpu.VMEM((1, 512), jnp.int32),
            pltpu.VMEM((1, 256), F32),
            pltpu.VMEM((4, 4608), jnp.int32),
            pltpu.VMEM((512, 512), BF16),
            pltpu.VMEM((4608, 512), BF16),
            pltpu.VMEM((2304, 512), BF16),
            pltpu.VMEM((2304, 512), BF16),
            pltpu.VMEM((2, 288, 512), BF16),
            pltpu.VMEM((2, 576, 512), BF16),
            pltpu.VMEM((576, 512), BF16),
            pltpu.VMEM((3, 144, 512), BF16),
            pltpu.VMEM((4608, 512), BF16),
            pltpu.VMEM((2, 576, 512), BF16),
            pltpu.VMEM((2, 1152, 512), BF16),
            pltpu.VMEM((1152, 512), BF16),
            pltpu.VMEM((576, 512), BF16),
            pltpu.SemaphoreType.DMA((14,)),
            pltpu.SemaphoreType.DMA((SEND_SLOTS,)),
            pltpu.SemaphoreType.DMA((7 * len(KV_WAVES) + 3 * len(Y_WAVES) + 1,)),
        ],
        compiler_params=pltpu.CompilerParams(
            collective_id=0, has_side_effects=True, vmem_limit_bytes=48 * 2**20
        ),
        cost_estimate=pl.CostEstimate(flops=5 * 10**9, bytes_accessed=15 * 10**6, transcendentals=0),
        name="reduce_both",
    )(token_counts, *(
        pltpu.with_memory_space_constraint(array, pltpu.HBM)
        for array in (
            hidden_in, kv_weight.reshape(8, 576, 512), kv_cotangent, block_signs.reshape(1, 512),
            level_table.reshape(1, 256), level_index,
        )
    ))
    return input_t.T, grad


def solution(mesh):
    return jax.shard_map(
        local,
        mesh=mesh,
        in_specs=(
            P("dp", None),
            P(None, "tensor"),
            P("dp", "tensor"),
            P("dp"),
            P("tensor"),
            P(),
            P("tensor", None),
        ),
        out_specs=(P("dp", "tensor"), P(None, "tensor")),
        check_vma=False,
    )
```

```python
import functools
import math

import jax
import jax.numpy as jnp
from jax import lax
from jax.experimental import pallas as pl
from jax.experimental.pallas import tpu as pltpu
from jax.sharding import PartitionSpec as P

MESH = pl.DeviceIdType.MESH
SEND_SLOTS = 16
F32 = jnp.float32
BF16 = jnp.bfloat16
HEAD = 128
NX, NZ, NY = 4, 4, 4

KV_WAVES = (1, 1, 1, 1, 1, 1, 1, 1, 1)
Y_WAVES = (64, 64, 64, 64, 64, 64, 64, 64, 64)


Z_DIRECT = (True, True, True, True, True, True, True, True, True)


def starts(sizes):
    out, at = [], 0
    for size in sizes:
        out.append(at)
        at += size
    return tuple(out)


KV_AT = starts(KV_WAVES)
Y_AT = starts(Y_WAVES)


ORDER = (
    ("encode", 0), ("partial", 0), ("encode", 1), ("pair", 0), ("encode", 2), ("partial", 2), ("encode", 3),
    ("pair", 1), ("encode", 4), ("encode", 5), ("x_mid", 0), ("partial", 3), ("pair", 3), ("partial", 5),
    ("encode", 6), ("x_mid", 1), ("pair", 4), ("x_end", 0), ("x_mid", 3), ("pair", 2), ("encode", 7),
    ("y_mid", 2), ("encode", 8), ("x_end", 1), ("x_mid", 4), ("pair", 6), ("partial", 8), ("x_end", 3),
    ("y_mid", 5), ("x_mid", 2), ("z_end", 0), ("pair", 5), ("pair", 8), ("x_end", 4), ("x_mid", 6),
    ("partial", 4), ("x_end", 2), ("pair", 7), ("z_end", 1), ("partial", 6), ("x_mid", 8), ("z_end", 3),
    ("x_mid", 5), ("x_end", 6), ("partial", 1), ("x_mid", 7), ("z_end", 4), ("x_own", 0), ("x_end", 8),
    ("y_mid", 0), ("x_own", 1), ("x_end", 5), ("y_mid", 1), ("x_own", 3), ("x_end", 7), ("y_mid", 8),
    ("z_end", 2), ("partial", 7), ("y_mid", 6), ("y_mid", 4), ("x_pass", 1), ("x_pass", 0), ("x_own", 4),
    ("z_end", 6), ("z_end", 8), ("y_mid", 3), ("z_end", 5), ("x_pass", 3), ("z_end", 7), ("x_own", 2),
    ("x_pass", 4), ("y_end", 0), ("x_own", 6), ("y_mid", 7), ("x_own", 8), ("y_end", 8), ("y_end", 1),
    ("y_end", 6), ("x_own", 5), ("y_end", 3), ("x_own", 7), ("y_end", 2), ("y_end", 5), ("y_end", 4),
    ("x_pass", 6), ("x_pass", 8), ("pair_last", 3), ("pair_last", 0), ("x_pass", 2), ("zl_end", 1),
    ("x_pass", 5), ("pair_last", 4), ("pair_last", 1), ("zl_end", 0), ("x_pass", 7), ("y_end", 7),
    ("pair_last", 2), ("pair_last", 6), ("zl_end", 2), ("pair_last", 8), ("pair_last", 5), ("pair_last", 7),
    ("zl_end", 6), ("zl_end", 3), ("zl_end", 8), ("zl_end", 4), ("zl_end", 5), ("zl_end", 7),
)


def rows_of(at, size):
    return pl.ds(pl.multiple_of(at, 16), size)


def add_rows(out, out_at, terms, size, block=32):
    block = min(block, size)

    def step(i, _):
        total = None
        for ref, at in terms:
            value = ref[rows_of(at + i * block, block), :].astype(F32)
            total = value if total is None else total + value
        out[rows_of(out_at + i * block, block), :] = total.astype(BF16)
        return 0

    lax.fori_loop(0, size // block, step, 0)


def kernel(
    count, hidden_hbm, weight_hbm, cot_hbm, signs_hbm, table_hbm, index_hbm,
    grad_out, input_out,
    hidden, weight, masked, signs, table, index, bt, enc, pair_in, summed,
    x_mid_in, x_in, x_sum, z_in, part, y_mid_in, y_in, y_sum, zl_in,
    local_sem, send_sem, recv_sem,
):
    dp, tensor = lax.axis_index("dp"), lax.axis_index("tensor")
    zh, x, core = dp // 8, (dp // 2) % 4, dp % 2
    y, zl = tensor // 2, tensor % 2

    def dp_of(zh_, x_, core_):
        return ((zh_ % 4) * 4 + (x_ % 4)) * 2 + core_

    def at_dp(zh_, x_, core_):
        return (dp_of(zh_, x_, core_), tensor)

    peer = at_dp(zh, x, 1 - core)
    x_next, x_prev = at_dp(zh, x + 1, core), at_dp(zh, x + 3, core)
    z_next, z_prev, z_far = at_dp(zh + 1, x, core), at_dp(zh + 3, x, core), at_dp(zh + 2, x, core)
    z_others = ((zh + 1, z_next), (zh + 3, z_prev), (zh + 2, z_far))
    y_next, y_prev = (dp, ((y + 1) % 4) * 2 + zl), (dp, ((y + 3) % 4) * 2 + zl)
    zl_peer = (dp, y * 2 + 1 - zl)
    neighbours = (peer, x_next, x_prev, z_next, z_prev, z_far, y_next, y_prev, zl_peer)

    local_used = [0]
    arrivals = {}
    slots = [0] * SEND_SLOTS
    slot = [0]

    def drain(semaphore, rows):
        view = enc.at[pl.ds(0, rows), :]
        pltpu.make_async_copy(view, view, semaphore).wait()

    def wait_for(key):
        index, rows = arrivals.pop(key)
        drain(recv_sem.at[index], rows)

    recv_of = {}

    def next_slot():
        slot[0] = (slot[0] + 1) % SEND_SLOTS
        if slots[slot[0]]:
            drain(send_sem.at[slot[0]], slots[slot[0]])
            slots[slot[0]] = 0

    def load(src, dst):
        copy = pltpu.make_async_copy(src, dst, local_sem.at[local_used[0]])
        local_used[0] += 1
        copy.start()
        return copy

    def send(src, dst, device, key):
        index = recv_of.setdefault(key, len(recv_of))
        rows = src.shape[0] * src.shape[1] // 512
        copy = pltpu.make_async_remote_copy(
            src_ref=src, dst_ref=dst, send_sem=send_sem.at[slot[0]], recv_sem=recv_sem.at[index],
            device_id=device, device_id_type=MESH,
        )
        copy.start()
        slots[slot[0]] += rows
        arrivals[key] = [index, arrivals.get(key, (0, 0))[1] + rows]

    cot_load = load(cot_hbm, masked)
    lanes = pl.ds(0, KV_WAVES[0] * 512)
    hidden_loads = [load(hidden_hbm.at[:, lanes], hidden.at[:, lanes])]
    barrier = pltpu.get_barrier_semaphore()
    for device in neighbours:
        pl.semaphore_signal(barrier, inc=1, device_id=device, device_id_type=MESH)
    small_loads = [load(signs_hbm, signs), load(table_hbm, table), load(index_hbm, index)]
    weight_loads = []

    def load_hidden(first, last):
        lanes = pl.ds(KV_AT[first] * 512, sum(KV_WAVES[first:last]) * 512)
        copy = load(hidden_hbm.at[:, lanes], hidden.at[:, lanes])
        hidden_loads.extend([copy] + [None] * (last - first - 1))

    def load_weight(v):
        rows = pl.ds(Y_AT[v], Y_WAVES[v])
        weight_loads.append(load(weight_hbm.at[:, rows, :], weight.at[:, rows, :]))

    load_weight(0)
    def load_rest():
        for w in range(1, len(KV_WAVES), 2):
            load_hidden(w, min(w + 2, len(KV_WAVES)))
            if len(weight_loads) < len(Y_WAVES):
                load_weight(len(weight_loads))
        while len(weight_loads) < len(Y_WAVES):
            load_weight(len(weight_loads))

    row_i = lax.broadcasted_iota(jnp.int32, (HEAD, HEAD), 0)
    col_i = lax.broadcasted_iota(jnp.int32, (HEAD, HEAD), 1)
    common = row_i & col_i
    common = common ^ (common >> 4)
    common = common ^ (common >> 2)
    common = common ^ (common >> 1)
    hadamard = (1 - 2 * (common & 1)).astype(F32)

    cot_load.wait()
    tokens = lax.broadcasted_iota(jnp.int32, (512, 512), 0)
    masked[...] = jnp.where(tokens < count[0], masked[...].astype(F32), 0.0).astype(BF16)
    for copy in small_loads:
        copy.wait()
    sign_row = (2 * signs[...] - 1).astype(F32)
    for j in range(4):
        lanes = pl.ds(j * HEAD, HEAD)
        turned = (hadamard * sign_row[:, j * HEAD:(j + 1) * HEAD]).astype(BF16)
        bt[lanes, :] = (
            lax.dot_general(turned, masked[:, lanes], (((1,), (1,)), ((), ())), preferred_element_type=F32)
            * (1.0 / 256.0)
        ).astype(BF16)

    def encode(w):
        if hidden_loads[w] is not None:
            hidden_loads[w].wait()

        def tile(i, _):
            at = pl.multiple_of((KV_AT[w] + i) * 512, 512)
            value = jnp.dot(bt[...], hidden[:, pl.ds(at, 512)], preferred_element_type=F32)
            low = jnp.broadcast_to(table[:, 0:128], (4, 128))
            high = jnp.broadcast_to(table[:, 128:256], (4, 128))
            bounds = []
            for k in range(4):
                ids = index[:, pl.ds(at + k * 128, 128)]
                first = jnp.take_along_axis(low, ids & 127, axis=1, mode="promise_in_bounds")
                second = jnp.take_along_axis(high, ids & 127, axis=1, mode="promise_in_bounds")
                bounds.append(jnp.where(ids >= 128, second, first))
            bound = jnp.concatenate(bounds, axis=1)
            for j in range(4):
                limit = bound[j:j + 1, :]
                clipped = jnp.clip(value[j * HEAD:(j + 1) * HEAD], -limit, limit).astype(BF16)
                enc[pl.ds(at, 512), pl.ds(j * HEAD, HEAD)] = clipped.T
            return 0

        lax.fori_loop(0, KV_WAVES[w], tile, 0)

    def own_rows(w, core_):
        g = KV_WAVES[w]
        return KV_AT[w] * 512 + core_ * 256 * g, 256 * g

    def pair_send(w):
        at, size = own_rows(w, 1 - core)
        send(enc.at[rows_of(at, size), :], pair_in.at[pl.ds(KV_AT[w] * 256, size), :], peer, ("pair", w))

    class Axis:
        def __init__(self, name, place, following, previous, source, mid_in, into):
            self.name, self.place, self.next, self.prev = name, place, following, previous
            self.source, self.mid_in, self.into = source, mid_in, into

        def piece(self, ref, base, chunk, half, h):
            return ref.at[rows_of(base + chunk * 2 * half + h * half, half), :]

        def begin(self, w, base, half, at):
            mid_rows = pl.ds(at // 2, half)
            here = functools.partial(self.piece, self.source, base)
            far, up, down = (self.place + 2) % 4, (self.place + 1) % 4, (self.place + 3) % 4
            send(here(far, half, 0), self.mid_in.at[0, mid_rows], self.next, (self.name, "mid", w))
            send(here(far, half, 1), self.mid_in.at[1, mid_rows], self.prev, (self.name, "mid", w))
            send(here(up, half, 1), self.piece(self.into.at[0], at, 0, half, 1), self.next, (self.name, "end", w))
            send(here(down, half, 0), self.piece(self.into.at[1], at, 0, half, 0), self.prev, (self.name, "end", w))

        def middle(self, w, base, half, at):
            up, down = (self.place + 1) % 4, (self.place + 3) % 4
            wait_for((self.name, "mid", w))
            for h, chunk, device in ((0, up, self.next), (1, down, self.prev)):
                first = base + chunk * 2 * half + h * half
                add_rows(self.source, first, ((self.source, first), (self.mid_in.at[h], at // 2)), half)
                send(
                    self.piece(self.source, base, chunk, half, h), self.piece(self.into.at[h], at, 0, half, h), device,
                    (self.name, "end", w),
                )

        def arrive(self, w):
            wait_for((self.name, "end", w))

    x_axis = Axis("x", x, x_next, x_prev, summed, x_mid_in, x_in)
    y_axis = Axis("y", y, y_next, y_prev, part, y_mid_in, y_in)

    def x_args(w):
        g = KV_WAVES[w]
        return KV_AT[w] * 256, 32 * g, KV_AT[w] * 64

    def z_args(w):
        g = KV_WAVES[w]
        return KV_AT[w] * 64, 16 * g

    def y_args(v):
        return 8 * Y_AT[v], Y_WAVES[v], 2 * Y_AT[v]

    def chunk_row(w, x_, zh_=None):
        g = KV_WAVES[w]
        row = KV_AT[w] * 512 + core * 256 * g + (x_ % 4) * 64 * g
        return row if zh_ is None else row + (zh_ % 4) * 16 * g

    def do_pair(w):
        wait_for(("pair", w))
        at, size = own_rows(w, core)
        add_rows(summed, KV_AT[w] * 256, ((enc, at), (pair_in, KV_AT[w] * 256)), size)
        x_axis.begin(w, *x_args(w))

    def do_x_end(w):
        x_axis.arrive(w)
        base, half, at = x_args(w)
        add_rows(
            x_sum, at, ((summed, base + x * 2 * half), (x_in.at[0], at), (x_in.at[1], at)), 2 * half
        )
        base, size = z_args(w)
        for i, (place, device) in enumerate(z_others):
            send(
                x_sum.at[rows_of(base + (place % 4) * size, size), :], z_in.at[i, pl.ds(KV_AT[w] * 16, size), :], device,
                ("z_end", w),
            )

    def do_z_end(w):
        wait_for(("z_end", w))
        base, half = z_args(w)
        rows = pl.ds(KV_AT[w] * 16, half)
        total = x_sum[rows_of(base + zh * half, half), :].astype(F32)
        for i in range(3):
            total = total + z_in[i, rows].astype(F32)
        requant = (total * (1.0 / math.sqrt(32.0))).astype(BF16)
        row = chunk_row(w, x, zh)
        for j in range(4):
            lanes = slice(j * HEAD, (j + 1) * HEAD)
            decoded = jnp.dot(requant[:, lanes], hadamard.astype(BF16), preferred_element_type=F32)
            grad_out[rows_of(row, half), lanes] = (
                decoded * (1.0 / math.sqrt(HEAD)) * sign_row[:, lanes]
            ).astype(BF16)
        whole = grad_out.at[rows_of(row, half), :]
        if Z_DIRECT[w]:
            for _, device in z_others:
                send(whole, whole, device, ("z_own", w))
        else:
            for _, device in z_others[:2]:
                send(whole, whole, device, ("z_first", w))

    def do_z_pass(w):
        half = 16 * KV_WAVES[w]
        wait_for(("z_first", w))
        for place, device, lanes in ((zh + 3, z_next, pl.ds(0, 256)), (zh + 1, z_prev, pl.ds(256, 256))):
            piece = grad_out.at[rows_of(chunk_row(w, x, place), half), lanes]
            send(piece, piece, device, ("z_own", w))

    def do_x_own(w):
        wait_for(("z_own", w))
        whole = grad_out.at[rows_of(chunk_row(w, x), 64 * KV_WAVES[w]), :]
        send(whole, whole, x_next, ("x_own", w))
        send(whole, whole, x_prev, ("x_own", w))
        send(whole, whole, peer, "last")

    def do_x_pass(w):
        half = 32 * KV_WAVES[w]
        wait_for(("x_own", w))
        for place, device, first in ((x + 3, x_next, 0), (x + 1, x_prev, half)):
            piece = grad_out.at[rows_of(chunk_row(w, place) + first, half), :]
            send(piece, piece, device, ("x_pass", w))
        for place in (x + 3, x + 1):
            whole = grad_out.at[rows_of(chunk_row(w, place), 2 * half), :]
            send(whole, whole, peer, "last")

    def do_pair_last(w):
        wait_for(("x_pass", w))
        whole = grad_out.at[rows_of(chunk_row(w, x + 2), 64 * KV_WAVES[w]), :]
        send(whole, whole, peer, "last")

    def partial(v):
        weight_loads[v].wait()
        size = Y_WAVES[v]

        def tile(i, _):
            rows = weight[pl.ds(i * 4, 4), pl.ds(Y_AT[v], size), :].reshape(4 * size, 512)
            part[rows_of(8 * Y_AT[v] + i * 4 * size, 4 * size), :] = lax.dot_general(
                rows, masked[...], (((1,), (1,)), ((), ())), preferred_element_type=F32
            ).astype(BF16)
            return 0

        lax.fori_loop(0, 2, tile, 0)

    def do_y_end(v):
        y_axis.arrive(v)
        base, half, at = y_args(v)
        add_rows(y_sum, at, ((part, base + y * 2 * half), (y_in.at[0], at), (y_in.at[1], at)), 2 * half)
        send(y_sum.at[rows_of(at + (1 - zl) * half, half), :], zl_in.at[pl.ds(Y_AT[v], half), :], zl_peer, ("zl", v))

    def do_zl_end(v):
        wait_for(("zl", v))
        base, half, at = y_args(v)
        total = (
            y_sum[rows_of(at + zl * half, half), :].astype(F32) + zl_in[pl.ds(Y_AT[v], half), :].astype(F32)
        ).astype(BF16)
        input_out[pl.ds(Y_AT[v], half), :] = total

    encode(0)
    partial(0)
    pl.semaphore_wait(barrier, len(neighbours))
    for name, w in ORDER:
        next_slot()
        if name == "encode":
            if w > 0:
                encode(w)
            pair_send(w)
        elif name == "pair":
            do_pair(w)
        elif name == "x_mid":
            x_axis.middle(w, *x_args(w))
        elif name == "x_end":
            do_x_end(w)
        elif name == "z_end":
            do_z_end(w)
        elif name == "z_pass":
            do_z_pass(w)
        elif name == "x_own":
            do_x_own(w)
        elif name == "x_pass":
            do_x_pass(w)
        elif name == "pair_last":
            do_pair_last(w)
        elif name == "partial":
            if w > 0:
                partial(w)
            y_axis.begin(w, *y_args(w))
            if w == 0:
                load_rest()
        elif name == "y_mid":
            y_axis.middle(w, *y_args(w))
        elif name == "y_end":
            do_y_end(w)
        elif name == "zl_end":
            do_zl_end(w)

    wait_for("last")
    for index, rows in enumerate(slots):
        if rows:
            drain(send_sem.at[index], rows)


def copy_out(grad, input_t, grad_out, input_out, sem):
    copies = [pltpu.make_async_copy(input_t, input_out, sem.at[0])]
    for i in range(8):
        rows = pl.ds(i * 576, 576)
        copies.append(pltpu.make_async_copy(grad.at[rows, :], grad_out.at[rows, :], sem.at[i + 1]))
    for copy in copies:
        copy.start()
    for copy in copies:
        copy.wait()


def local(hidden_in, kv_weight, kv_cotangent, token_counts, block_signs, level_table, level_index):
    hbm = pl.BlockSpec(memory_space=pltpu.HBM)
    vmem = pl.BlockSpec(memory_space=pltpu.VMEM)
    grad, input_t = pl.pallas_call(
        kernel,
        out_shape=(
            jax.ShapeDtypeStruct((4608, 512), BF16),
            jax.ShapeDtypeStruct((576, 512), BF16),
        ),
        in_specs=[pl.BlockSpec(memory_space=pltpu.SMEM)] + [hbm] * 6,
        out_specs=(vmem, vmem),
        scratch_shapes=[
            pltpu.VMEM((512, 4608), BF16),
            pltpu.VMEM((8, 576, 512), BF16),
            pltpu.VMEM((512, 512), BF16),
            pltpu.VMEM((1, 512), jnp.int32),
            pltpu.VMEM((1, 256), F32),
            pltpu.VMEM((4, 4608), jnp.int32),
            pltpu.VMEM((512, 512), BF16),
            pltpu.VMEM((4608, 512), BF16),
            pltpu.VMEM((2304, 512), BF16),
            pltpu.VMEM((2304, 512), BF16),
            pltpu.VMEM((2, 288, 512), BF16),
            pltpu.VMEM((2, 576, 512), BF16),
            pltpu.VMEM((576, 512), BF16),
            pltpu.VMEM((3, 144, 512), BF16),
            pltpu.VMEM((4608, 512), BF16),
            pltpu.VMEM((2, 576, 512), BF16),
            pltpu.VMEM((2, 1152, 512), BF16),
            pltpu.VMEM((1152, 512), BF16),
            pltpu.VMEM((576, 512), BF16),
            pltpu.SemaphoreType.DMA((9 + len(Y_WAVES),)),
            pltpu.SemaphoreType.DMA((SEND_SLOTS,)),
            pltpu.SemaphoreType.DMA((7 * len(KV_WAVES) + Z_DIRECT.count(False) + 3 * len(Y_WAVES) + 1,)),
        ],
        compiler_params=pltpu.CompilerParams(
            collective_id=0, has_side_effects=True, vmem_limit_bytes=48 * 2**20
        ),
        cost_estimate=pl.CostEstimate(flops=5 * 10**9, bytes_accessed=15 * 10**6, transcendentals=0),
        name="reduce_both",
    )(token_counts, *(
        pltpu.with_memory_space_constraint(array, pltpu.HBM)
        for array in (
            hidden_in, kv_weight.reshape(8, 576, 512), kv_cotangent, block_signs.reshape(1, 512),
            level_table.reshape(1, 256), level_index,
        )
    ))
    grad, input_t = pl.pallas_call(
        copy_out,
        out_shape=(jax.ShapeDtypeStruct((4608, 512), BF16), jax.ShapeDtypeStruct((576, 512), BF16)),
        in_specs=[pl.BlockSpec(memory_space=pl.ANY)] * 2,
        out_specs=(hbm, hbm),
        scratch_shapes=[pltpu.SemaphoreType.DMA((9,))],
        compiler_params=pltpu.CompilerParams(vmem_limit_bytes=2**20),
        name="copy_out",
    )(pltpu.with_memory_space_constraint(grad, pltpu.VMEM), pltpu.with_memory_space_constraint(input_t, pltpu.VMEM))
    return input_t.T, grad


def solution(mesh):
    return jax.shard_map(
        local,
        mesh=mesh,
        in_specs=(
            P("dp", None),
            P(None, "tensor"),
            P("dp", "tensor"),
            P("dp"),
            P("tensor"),
            P(),
            P("tensor", None),
        ),
        out_specs=(P("dp", "tensor"), P(None, "tensor")),
        check_vma=False,
    )
```

```python
import functools
import math

import jax
import jax.numpy as jnp
from jax import lax
from jax.experimental import pallas as pl
from jax.experimental.pallas import tpu as pltpu
from jax.sharding import PartitionSpec as P

MESH = pl.DeviceIdType.MESH
SEND_SLOTS = 16
F32 = jnp.float32
BF16 = jnp.bfloat16
HEAD = 128
NX, NZ, NY = 4, 4, 4

KV_WAVES = (1, 1, 1, 1, 1, 1, 1, 1, 1)
Y_WAVES = (64, 64, 64, 64, 64, 64, 64, 64, 32, 32)


Z_DIRECT = (False, False, True, True, True, True, True, True, True)
X_DIRECT = (False, False, False, False, False, False, False, False, False)


def starts(sizes):
    out, at = [], 0
    for size in sizes:
        out.append(at)
        at += size
    return tuple(out)


KV_AT = starts(KV_WAVES)
Y_AT = starts(Y_WAVES)


ORDER = (
    ("encode", 0), ("partial", 0), ("encode", 1), ("pair", 0), ("encode", 2), ("encode", 3), ("pair", 1),
    ("partial", 4), ("partial", 1), ("pair", 2), ("encode", 4), ("partial", 6), ("x_mid", 0), ("pair", 3),
    ("encode", 5), ("encode", 6), ("x_mid", 1), ("encode", 7), ("encode", 8), ("x_mid", 2), ("pair", 4),
    ("x_end", 0), ("partial", 9), ("x_mid", 3), ("pair", 8), ("x_end", 1), ("x_end", 2), ("x_mid", 4),
    ("partial", 5), ("x_end", 3), ("x_mid", 8), ("z_end", 0), ("pair", 5), ("pair", 6), ("x_end", 4),
    ("pair", 7), ("z_end", 1), ("partial", 3), ("y_mid", 4), ("x_end", 8), ("z_end", 2), ("x_mid", 5),
    ("z_pass", 0), ("x_mid", 6), ("partial", 2), ("z_end", 3), ("partial", 7), ("x_mid", 7), ("x_end", 5),
    ("y_mid", 1), ("y_mid", 5), ("z_pass", 1), ("x_end", 6), ("x_own", 2), ("x_end", 7), ("z_end", 4),
    ("y_mid", 9), ("x_own", 0), ("z_end", 8), ("x_own", 3), ("x_own", 1), ("z_end", 5), ("x_pass", 2),
    ("partial", 8), ("y_mid", 6), ("x_pass", 0), ("z_end", 6), ("y_mid", 3), ("x_pass", 3), ("y_mid", 0),
    ("z_end", 7), ("x_own", 4), ("x_pass", 1), ("y_end", 4), ("y_mid", 2), ("y_end", 1), ("y_end", 9),
    ("pair_last", 2), ("x_own", 8), ("y_mid", 8), ("x_own", 5), ("x_own", 6), ("y_mid", 7), ("y_end", 5),
    ("pair_last", 0), ("x_own", 7), ("y_end", 3), ("y_end", 2), ("zl_end", 4), ("x_pass", 4), ("y_end", 8),
    ("y_end", 6), ("x_pass", 5), ("pair_last", 3), ("x_pass", 8), ("x_pass", 6), ("y_end", 7), ("x_pass", 7),
    ("y_end", 0), ("pair_last", 1), ("zl_end", 1), ("pair_last", 5), ("zl_end", 3), ("pair_last", 4),
    ("pair_last", 8), ("pair_last", 6), ("zl_end", 8), ("zl_end", 9), ("pair_last", 7), ("zl_end", 2),
    ("zl_end", 7), ("zl_end", 5), ("zl_end", 6), ("zl_end", 0),
)


def rows_of(at, size):
    return pl.ds(pl.multiple_of(at, 16), size)


def add_rows(out, out_at, terms, size, block=32):
    block = min(block, size)

    def step(i, _):
        total = None
        for ref, at in terms:
            value = ref[rows_of(at + i * block, block), :].astype(F32)
            total = value if total is None else total + value
        out[rows_of(out_at + i * block, block), :] = total.astype(BF16)
        return 0

    lax.fori_loop(0, size // block, step, 0)


def kernel(
    count, hidden_hbm, weight_hbm, cot_hbm, signs_hbm, table_hbm, index_hbm,
    grad_out, input_out,
    hidden, weight, masked, signs, table, index, bt, enc, pair_in, summed,
    x_mid_in, x_in, x_sum, z_in, part, y_mid_in, y_in, y_sum, zl_in,
    local_sem, send_sem, recv_sem,
):
    dp, tensor = lax.axis_index("dp"), lax.axis_index("tensor")
    zh, x, core = dp // 8, (dp // 2) % 4, dp % 2
    y, zl = tensor // 2, tensor % 2

    def dp_of(zh_, x_, core_):
        return ((zh_ % 4) * 4 + (x_ % 4)) * 2 + core_

    def at_dp(zh_, x_, core_):
        return (dp_of(zh_, x_, core_), tensor)

    peer = at_dp(zh, x, 1 - core)
    x_next, x_prev = at_dp(zh, x + 1, core), at_dp(zh, x + 3, core)
    x_far = at_dp(zh, x + 2, core)
    x_others = ((x + 1, x_next), (x + 3, x_prev), (x + 2, x_far))
    z_next, z_prev, z_far = at_dp(zh + 1, x, core), at_dp(zh + 3, x, core), at_dp(zh + 2, x, core)
    z_others = ((zh + 1, z_next), (zh + 3, z_prev), (zh + 2, z_far))
    y_next, y_prev = (dp, ((y + 1) % 4) * 2 + zl), (dp, ((y + 3) % 4) * 2 + zl)
    zl_peer = (dp, y * 2 + 1 - zl)
    neighbours = (peer, x_next, x_prev, x_far, z_next, z_prev, z_far, y_next, y_prev, zl_peer)

    local_used = [0]
    arrivals = {}
    slots = [0] * SEND_SLOTS
    slot = [0]

    def drain(semaphore, rows):
        view = enc.at[pl.ds(0, rows), :]
        pltpu.make_async_copy(view, view, semaphore).wait()

    def wait_for(key):
        index, rows = arrivals.pop(key)
        drain(recv_sem.at[index], rows)

    recv_of = {}

    def next_slot():
        slot[0] = (slot[0] + 1) % SEND_SLOTS
        if slots[slot[0]]:
            drain(send_sem.at[slot[0]], slots[slot[0]])
            slots[slot[0]] = 0

    def load(src, dst):
        copy = pltpu.make_async_copy(src, dst, local_sem.at[local_used[0]])
        local_used[0] += 1
        copy.start()
        return copy

    def send(src, dst, device, key):
        index = recv_of.setdefault(key, len(recv_of))
        rows = src.shape[0] * src.shape[1] // 512
        copy = pltpu.make_async_remote_copy(
            src_ref=src, dst_ref=dst, send_sem=send_sem.at[slot[0]], recv_sem=recv_sem.at[index],
            device_id=device, device_id_type=MESH,
        )
        copy.start()
        slots[slot[0]] += rows
        arrivals[key] = [index, arrivals.get(key, (0, 0))[1] + rows]

    cot_load = load(cot_hbm, masked)
    lanes = pl.ds(0, KV_WAVES[0] * 512)
    hidden_loads = [load(hidden_hbm.at[:, lanes], hidden.at[:, lanes])]
    barrier = pltpu.get_barrier_semaphore()
    for device in neighbours:
        pl.semaphore_signal(barrier, inc=1, device_id=device, device_id_type=MESH)
    small_loads = [load(signs_hbm, signs), load(table_hbm, table), load(index_hbm, index)]
    weight_loads = []

    def load_hidden(first, last):
        lanes = pl.ds(KV_AT[first] * 512, sum(KV_WAVES[first:last]) * 512)
        copy = load(hidden_hbm.at[:, lanes], hidden.at[:, lanes])
        hidden_loads.extend([copy] + [None] * (last - first - 1))

    def load_weight(v):
        rows = pl.ds(Y_AT[v], Y_WAVES[v])
        weight_loads.append(load(weight_hbm.at[:, rows, :], weight.at[:, rows, :]))

    load_weight(0)
    def load_rest():
        for w in range(1, len(KV_WAVES), 2):
            load_hidden(w, min(w + 2, len(KV_WAVES)))
            if len(weight_loads) < len(Y_WAVES):
                load_weight(len(weight_loads))
        while len(weight_loads) < len(Y_WAVES):
            load_weight(len(weight_loads))

    row_i = lax.broadcasted_iota(jnp.int32, (HEAD, HEAD), 0)
    col_i = lax.broadcasted_iota(jnp.int32, (HEAD, HEAD), 1)
    common = row_i & col_i
    common = common ^ (common >> 4)
    common = common ^ (common >> 2)
    common = common ^ (common >> 1)
    hadamard = (1 - 2 * (common & 1)).astype(F32)

    cot_load.wait()
    tokens = lax.broadcasted_iota(jnp.int32, (512, 512), 0)
    masked[...] = jnp.where(tokens < count[0], masked[...].astype(F32), 0.0).astype(BF16)
    for copy in small_loads:
        copy.wait()
    sign_row = (2 * signs[...] - 1).astype(F32)
    for j in range(4):
        lanes = pl.ds(j * HEAD, HEAD)
        turned = (hadamard * sign_row[:, j * HEAD:(j + 1) * HEAD]).astype(BF16)
        bt[lanes, :] = (
            lax.dot_general(turned, masked[:, lanes], (((1,), (1,)), ((), ())), preferred_element_type=F32)
            * (1.0 / 256.0)
        ).astype(BF16)

    def encode(w):
        if hidden_loads[w] is not None:
            hidden_loads[w].wait()

        def tile(i, _):
            at = pl.multiple_of((KV_AT[w] + i) * 512, 512)
            value = jnp.dot(bt[...], hidden[:, pl.ds(at, 512)], preferred_element_type=F32)
            low = jnp.broadcast_to(table[:, 0:128], (4, 128))
            high = jnp.broadcast_to(table[:, 128:256], (4, 128))
            bounds = []
            for k in range(4):
                ids = index[:, pl.ds(at + k * 128, 128)]
                first = jnp.take_along_axis(low, ids & 127, axis=1, mode="promise_in_bounds")
                second = jnp.take_along_axis(high, ids & 127, axis=1, mode="promise_in_bounds")
                bounds.append(jnp.where(ids >= 128, second, first))
            bound = jnp.concatenate(bounds, axis=1)
            for j in range(4):
                limit = bound[j:j + 1, :]
                clipped = jnp.clip(value[j * HEAD:(j + 1) * HEAD], -limit, limit).astype(BF16)
                enc[pl.ds(at, 512), pl.ds(j * HEAD, HEAD)] = clipped.T
            return 0

        lax.fori_loop(0, KV_WAVES[w], tile, 0)

    def own_rows(w, core_):
        g = KV_WAVES[w]
        return KV_AT[w] * 512 + core_ * 256 * g, 256 * g

    def pair_send(w):
        at, size = own_rows(w, 1 - core)
        send(enc.at[rows_of(at, size), :], pair_in.at[pl.ds(KV_AT[w] * 256, size), :], peer, ("pair", w))

    class Axis:
        def __init__(self, name, place, following, previous, source, mid_in, into):
            self.name, self.place, self.next, self.prev = name, place, following, previous
            self.source, self.mid_in, self.into = source, mid_in, into

        def piece(self, ref, base, chunk, half, h):
            return ref.at[rows_of(base + chunk * 2 * half + h * half, half), :]

        def begin(self, w, base, half, at):
            mid_rows = pl.ds(at // 2, half)
            here = functools.partial(self.piece, self.source, base)
            far, up, down = (self.place + 2) % 4, (self.place + 1) % 4, (self.place + 3) % 4
            send(here(far, half, 0), self.mid_in.at[0, mid_rows], self.next, (self.name, "mid", w))
            send(here(far, half, 1), self.mid_in.at[1, mid_rows], self.prev, (self.name, "mid", w))
            send(here(up, half, 1), self.piece(self.into.at[0], at, 0, half, 1), self.next, (self.name, "end", w))
            send(here(down, half, 0), self.piece(self.into.at[1], at, 0, half, 0), self.prev, (self.name, "end", w))

        def middle(self, w, base, half, at):
            up, down = (self.place + 1) % 4, (self.place + 3) % 4
            wait_for((self.name, "mid", w))
            for h, chunk, device in ((0, up, self.next), (1, down, self.prev)):
                first = base + chunk * 2 * half + h * half
                add_rows(self.source, first, ((self.source, first), (self.mid_in.at[h], at // 2)), half)
                send(
                    self.piece(self.source, base, chunk, half, h), self.piece(self.into.at[h], at, 0, half, h), device,
                    (self.name, "end", w),
                )

        def arrive(self, w):
            wait_for((self.name, "end", w))

    x_axis = Axis("x", x, x_next, x_prev, summed, x_mid_in, x_in)
    y_axis = Axis("y", y, y_next, y_prev, part, y_mid_in, y_in)

    def x_args(w):
        g = KV_WAVES[w]
        return KV_AT[w] * 256, 32 * g, KV_AT[w] * 64

    def z_args(w):
        g = KV_WAVES[w]
        return KV_AT[w] * 64, 16 * g

    def y_args(v):
        return 8 * Y_AT[v], Y_WAVES[v], 2 * Y_AT[v]

    def chunk_row(w, x_, zh_=None):
        g = KV_WAVES[w]
        row = KV_AT[w] * 512 + core * 256 * g + (x_ % 4) * 64 * g
        return row if zh_ is None else row + (zh_ % 4) * 16 * g

    def do_pair(w):
        wait_for(("pair", w))
        at, size = own_rows(w, core)
        add_rows(summed, KV_AT[w] * 256, ((enc, at), (pair_in, KV_AT[w] * 256)), size)
        if not X_DIRECT[w]:
            x_axis.begin(w, *x_args(w))
            return
        base, half, at = x_args(w)
        for i, (place, device) in enumerate(x_others):
            send(
                summed.at[rows_of(base + (place % 4) * 2 * half, 2 * half), :], x_in.at[i, pl.ds(at, 2 * half), :], device,
                ("x", "end", w),
            )

    def do_x_end(w):
        x_axis.arrive(w)
        base, half, at = x_args(w)
        terms = [(summed, base + x * 2 * half)] + [(x_in.at[i], at) for i in range(3 if X_DIRECT[w] else 2)]
        add_rows(x_sum, at, terms, 2 * half)
        base, size = z_args(w)
        for i, (place, device) in enumerate(z_others):
            send(
                x_sum.at[rows_of(base + (place % 4) * size, size), :], z_in.at[i, pl.ds(KV_AT[w] * 16, size), :], device,
                ("z_end", w),
            )

    def do_z_end(w):
        wait_for(("z_end", w))
        base, half = z_args(w)
        rows = pl.ds(KV_AT[w] * 16, half)
        total = x_sum[rows_of(base + zh * half, half), :].astype(F32)
        for i in range(3):
            total = total + z_in[i, rows].astype(F32)
        requant = (total * (1.0 / math.sqrt(32.0))).astype(BF16)
        row = chunk_row(w, x, zh)
        for j in range(4):
            lanes = slice(j * HEAD, (j + 1) * HEAD)
            decoded = jnp.dot(requant[:, lanes], hadamard.astype(BF16), preferred_element_type=F32)
            grad_out[rows_of(row, half), lanes] = (
                decoded * (1.0 / math.sqrt(HEAD)) * sign_row[:, lanes]
            ).astype(BF16)
        whole = grad_out.at[rows_of(row, half), :]
        if Z_DIRECT[w]:
            for _, device in z_others:
                send(whole, whole, device, ("z_own", w))
        else:
            for _, device in z_others[:2]:
                send(whole, whole, device, ("z_first", w))

    def do_z_pass(w):
        half = 16 * KV_WAVES[w]
        wait_for(("z_first", w))
        for place, device, lanes in ((zh + 3, z_next, pl.ds(0, 256)), (zh + 1, z_prev, pl.ds(256, 256))):
            piece = grad_out.at[rows_of(chunk_row(w, x, place), half), lanes]
            send(piece, piece, device, ("z_own", w))

    def do_x_own(w):
        wait_for(("z_own", w))
        whole = grad_out.at[rows_of(chunk_row(w, x), 64 * KV_WAVES[w]), :]
        send(whole, whole, x_next, ("x_own", w))
        send(whole, whole, x_prev, ("x_own", w))
        send(whole, whole, peer, "last")

    def do_x_pass(w):
        half = 32 * KV_WAVES[w]
        wait_for(("x_own", w))
        for place, device, first in ((x + 3, x_next, 0), (x + 1, x_prev, half)):
            piece = grad_out.at[rows_of(chunk_row(w, place) + first, half), :]
            send(piece, piece, device, ("x_pass", w))
        for place in (x + 3, x + 1):
            whole = grad_out.at[rows_of(chunk_row(w, place), 2 * half), :]
            send(whole, whole, peer, "last")

    def do_pair_last(w):
        wait_for(("x_pass", w))
        whole = grad_out.at[rows_of(chunk_row(w, x + 2), 64 * KV_WAVES[w]), :]
        send(whole, whole, peer, "last")

    def partial(v):
        weight_loads[v].wait()
        size = Y_WAVES[v]

        def tile(i, _):
            rows = weight[pl.ds(i * 4, 4), pl.ds(Y_AT[v], size), :].reshape(4 * size, 512)
            part[rows_of(8 * Y_AT[v] + i * 4 * size, 4 * size), :] = lax.dot_general(
                rows, masked[...], (((1,), (1,)), ((), ())), preferred_element_type=F32
            ).astype(BF16)
            return 0

        lax.fori_loop(0, 2, tile, 0)

    def do_y_end(v):
        y_axis.arrive(v)
        base, half, at = y_args(v)
        add_rows(y_sum, at, ((part, base + y * 2 * half), (y_in.at[0], at), (y_in.at[1], at)), 2 * half)
        send(y_sum.at[rows_of(at + (1 - zl) * half, half), :], zl_in.at[pl.ds(Y_AT[v], half), :], zl_peer, ("zl", v))

    def do_zl_end(v):
        wait_for(("zl", v))
        base, half, at = y_args(v)
        total = (
            y_sum[rows_of(at + zl * half, half), :].astype(F32) + zl_in[pl.ds(Y_AT[v], half), :].astype(F32)
        ).astype(BF16)
        input_out[pl.ds(Y_AT[v], half), :] = total

    encode(0)
    partial(0)
    pl.semaphore_wait(barrier, len(neighbours))
    for name, w in ORDER:
        next_slot()
        if name == "encode":
            if w > 0:
                encode(w)
            pair_send(w)
        elif name == "pair":
            do_pair(w)
        elif name == "x_mid":
            x_axis.middle(w, *x_args(w))
        elif name == "x_end":
            do_x_end(w)
        elif name == "z_end":
            do_z_end(w)
        elif name == "z_pass":
            do_z_pass(w)
        elif name == "x_own":
            do_x_own(w)
        elif name == "x_pass":
            do_x_pass(w)
        elif name == "pair_last":
            do_pair_last(w)
        elif name == "partial":
            if w > 0:
                partial(w)
            y_axis.begin(w, *y_args(w))
            if w == 0:
                load_rest()
        elif name == "y_mid":
            y_axis.middle(w, *y_args(w))
        elif name == "y_end":
            do_y_end(w)
        elif name == "zl_end":
            do_zl_end(w)

    wait_for("last")
    for index, rows in enumerate(slots):
        if rows:
            drain(send_sem.at[index], rows)


def copy_out(grad, input_t, grad_out, input_out, sem):
    copies = [pltpu.make_async_copy(input_t, input_out, sem.at[0])]
    for i in range(8):
        rows = pl.ds(i * 576, 576)
        copies.append(pltpu.make_async_copy(grad.at[rows, :], grad_out.at[rows, :], sem.at[i + 1]))
    for copy in copies:
        copy.start()
    for copy in copies:
        copy.wait()


def local(hidden_in, kv_weight, kv_cotangent, token_counts, block_signs, level_table, level_index):
    hbm = pl.BlockSpec(memory_space=pltpu.HBM)
    vmem = pl.BlockSpec(memory_space=pltpu.VMEM)
    grad, input_t = pl.pallas_call(
        kernel,
        out_shape=(
            jax.ShapeDtypeStruct((4608, 512), BF16),
            jax.ShapeDtypeStruct((576, 512), BF16),
        ),
        in_specs=[pl.BlockSpec(memory_space=pltpu.SMEM)] + [hbm] * 6,
        out_specs=(vmem, vmem),
        scratch_shapes=[
            pltpu.VMEM((512, 4608), BF16),
            pltpu.VMEM((8, 576, 512), BF16),
            pltpu.VMEM((512, 512), BF16),
            pltpu.VMEM((1, 512), jnp.int32),
            pltpu.VMEM((1, 256), F32),
            pltpu.VMEM((4, 4608), jnp.int32),
            pltpu.VMEM((512, 512), BF16),
            pltpu.VMEM((4608, 512), BF16),
            pltpu.VMEM((2304, 512), BF16),
            pltpu.VMEM((2304, 512), BF16),
            pltpu.VMEM((2, 288, 512), BF16),
            pltpu.VMEM((3, 576, 512), BF16),
            pltpu.VMEM((576, 512), BF16),
            pltpu.VMEM((3, 144, 512), BF16),
            pltpu.VMEM((4608, 512), BF16),
            pltpu.VMEM((2, 576, 512), BF16),
            pltpu.VMEM((2, 1152, 512), BF16),
            pltpu.VMEM((1152, 512), BF16),
            pltpu.VMEM((576, 512), BF16),
            pltpu.SemaphoreType.DMA((9 + len(Y_WAVES),)),
            pltpu.SemaphoreType.DMA((SEND_SLOTS,)),
            pltpu.SemaphoreType.DMA((7 * len(KV_WAVES) + Z_DIRECT.count(False) + 3 * len(Y_WAVES) + 1,)),
        ],
        compiler_params=pltpu.CompilerParams(
            collective_id=0, has_side_effects=True, vmem_limit_bytes=48 * 2**20
        ),
        cost_estimate=pl.CostEstimate(flops=5 * 10**9, bytes_accessed=15 * 10**6, transcendentals=0),
        name="reduce_both",
    )(token_counts, *(
        pltpu.with_memory_space_constraint(array, pltpu.HBM)
        for array in (
            hidden_in, kv_weight.reshape(8, 576, 512), kv_cotangent, block_signs.reshape(1, 512),
            level_table.reshape(1, 256), level_index,
        )
    ))
    grad, input_t = pl.pallas_call(
        copy_out,
        out_shape=(jax.ShapeDtypeStruct((4608, 512), BF16), jax.ShapeDtypeStruct((576, 512), BF16)),
        in_specs=[pl.BlockSpec(memory_space=pl.ANY)] * 2,
        out_specs=(hbm, hbm),
        scratch_shapes=[pltpu.SemaphoreType.DMA((9,))],
        compiler_params=pltpu.CompilerParams(vmem_limit_bytes=2**20),
        name="copy_out",
    )(pltpu.with_memory_space_constraint(grad, pltpu.VMEM), pltpu.with_memory_space_constraint(input_t, pltpu.VMEM))
    return input_t.T, grad


def solution(mesh):
    return jax.shard_map(
        local,
        mesh=mesh,
        in_specs=(
            P("dp", None),
            P(None, "tensor"),
            P("dp", "tensor"),
            P("dp"),
            P("tensor"),
            P(),
            P("tensor", None),
        ),
        out_specs=(P("dp", "tensor"), P(None, "tensor")),
        check_vma=False,
    )
```
